32 devices in a mesh: lat: 2 (over x), lon: 16 (over z, y, core).
Axes of the slice: x: 2, y: 2, z: 4, core: 2. Of those that a mesh axis runs over, the one named last changes fastest.
Arguments:
- fields: bfloat16 [16, 512, 768], P('lat', 'lon'), may hold values from -60 to 60
- conv_kernel: float32 [3, 3, 768], replicated, may hold values from -1 to 1
- layer_norm_gain: float32 [768], replicated, may hold values from 0.1 to 1.9
- qkv_weight: bfloat16 [768, 2304], replicated, may hold values from -0.21875 to 0.21875
- out_weight: bfloat16 [768, 768], replicated, may hold values from -0.21875 to 0.21875
- score_bias: float32 [24, 64, 64], replicated, may hold values from -4 to 400
- pattern: int32 [2, 16, 256], P('lat', 'lon'), may hold values from 0 to 255, each once within a row
- cotangent: bfloat16 [16, 512, 768], P('lat', 'lon'), may hold values from -6 to 6
Outputs:
- block_out: bfloat16 [16, 512, 768], P('lat', 'lon')
- grad_fields: bfloat16 [16, 512, 768], P('lat', 'lon')
- grad_project: float32 [768, 768], P('lat', 'lon')
- grad_kernel: float32 [3, 3, 768], replicated
- gain_gradient: float32 [768], replicated
The draws below stay inside these ranges and needn't reach their ends.
Inputs may be any that keep to these rules, and one draw needn't show every extreme that they name: pattern[a, b, :] lists each of the 256 cells of block (a, b) once.
All inputs are finite; a program needn't handle non-finite values.
Results may differ from the reference program's by a relative error of at most 0.028.
Values may be sent and summed in bfloat16 or wider, within the bound.
No kernel may reach another device: no remote copies, remote signals or barrier semaphores. Data moves between devices by JAX's collectives and lax.ppermute only.
A program may use at most 128 MiB of HBM per device.

```python
import math
import jax
import jax.numpy as jnp
from jax import lax

LAT_DEV = 8
LON_DEV = 32
HEADS = 24
HEAD_DIM = 32
GROUP = 64
D = 768
LATS = 16
LONS = 512
CELLS_DEV = 256
BLOCKS = 32
SLOTS = 8
TOKENS = 8192
N_LAT = 2
N_LON = 16


def draw_fields(key, part):
    base = jax.random.normal(jax.random.fold_in(key, 11), (LATS, LONS, D), jnp.float32)
    return jnp.clip(base, -6.0, 6.0).astype(jnp.bfloat16)


def draw_score_bias(key, part):
    return jnp.clip(jax.random.normal(jax.random.fold_in(key, 26), (HEADS, GROUP, GROUP), jnp.float32), -4.0, 4.0)


def shard_levels(stream_key, extent, split, low, high):
    factor_of, own = 1.0, jax.random.fold_in(stream_key, 6)
    for axis_at, shards_of in split:
        draws = jnp.exp(jax.random.uniform(jax.random.fold_in(own, axis_at), (shards_of,), jnp.float32, low / len(split), high / len(split)))
        factor_of = factor_of * jnp.repeat(draws, extent[axis_at] // shards_of).reshape([-1 if axis == axis_at else 1 for axis in range(len(extent))])
    return factor_of


def gaussian(own_key, shape, width, limit, split=(), kind=jnp.bfloat16):
    drawn = width * jax.random.normal(own_key, shape, jnp.float32)
    if split:
        drawn = drawn * shard_levels(own_key, shape, split, -0.22, 0.18)
    return jnp.clip(drawn, -limit, limit).astype(kind)


def setup_inputs(seed: int = 0) -> dict:
    arg_keys = jax.random.split(jax.random.key(seed), 9)
    fields = draw_fields(jax.random.fold_in(arg_keys[8], 71), 0)
    conv_kernel = gaussian(arg_keys[1], (3, 3, D), 0.25, 1.0, (), jnp.float32)
    layer_norm_gain = jnp.clip(1.0 + 0.18 * jax.random.normal(arg_keys[2], (D,), jnp.float32), 0.1, 1.9)
    qkv_weight = gaussian(arg_keys[3], (D, 3 * D), D ** -0.5, 0.21875)
    out_weight = gaussian(arg_keys[4], (D, D), D ** -0.5, 0.21875)
    score_bias = draw_score_bias(jax.random.fold_in(arg_keys[8], 71), 0)
    pattern = jax.vmap(lambda own: jax.random.permutation(own, CELLS_DEV))(jax.random.split(arg_keys[6], N_LAT * N_LON)).reshape((N_LAT, N_LON, CELLS_DEV)).astype(jnp.int32)
    cotangent = gaussian(arg_keys[7], (LATS, LONS, D), 1.0, 6.0, ((0, 2), (1, 16)))
    return {"fields": fields, "conv_kernel": conv_kernel, "layer_norm_gain": layer_norm_gain, "qkv_weight": qkv_weight, "out_weight": out_weight, "score_bias": score_bias, "pattern": pattern, "cotangent": cotangent}


epsilon = 1e-05

def spread(field):
    padded = jnp.pad(field, ((1, 1), (0, 0), (0, 0)))
    return jnp.concatenate([padded[:, -1:], padded, padded[:, :1]], axis=1)

def apply_taps(padded, conv_kernel, lat_rows, lon_cols):
    summed = jnp.zeros((lat_rows, lon_cols, padded.shape[2]), jnp.float32)
    for lat_tap in range(3):
        for lon_tap in range(3):
            summed = summed + conv_kernel[lat_tap, lon_tap] * padded[lat_tap:lat_tap + lat_rows, lon_tap:lon_tap + lon_cols]
    return summed

def to_owner(field, pattern):
    chans = field.shape[-1]
    blocked = field.reshape(N_LAT, LAT_DEV, N_LON, LON_DEV, chans).transpose(0, 2, 1, 3, 4)
    blocked = blocked.reshape(N_LAT, N_LON, CELLS_DEV, chans)
    slotted = jnp.take_along_axis(blocked, pattern[..., None], axis=2)
    slotted = slotted.reshape(N_LAT, N_LON, N_LAT, N_LON, SLOTS, chans).transpose(2, 3, 4, 0, 1, 5)
    return slotted.reshape(BLOCKS, CELLS_DEV, chans)

def to_grid(grouped, inverse):
    chans = grouped.shape[-1]
    slotted = grouped.reshape(N_LAT, N_LON, SLOTS, N_LAT, N_LON, chans).transpose(3, 4, 0, 1, 2, 5)
    slotted = slotted.reshape(N_LAT, N_LON, CELLS_DEV, chans)
    blocked = jnp.take_along_axis(slotted, inverse[..., None], axis=2)
    blocked = blocked.reshape(N_LAT, N_LON, LAT_DEV, LON_DEV, chans).transpose(0, 2, 1, 3, 4)
    return blocked.reshape(LATS, LONS, chans)

def attention_probs(queries, key_rows, score_bias):
    scores = jnp.einsum('gihd,gjhd->ghij', queries.astype(jnp.float32), key_rows.astype(jnp.float32))
    scores = scores * HEAD_DIM ** (-0.5) + score_bias[None]
    peak = lax.optimization_barrier(jnp.max(scores, axis=-1, keepdims=True))
    lifted = jnp.exp(scores - peak)
    return lifted / lax.optimization_barrier(jnp.sum(lifted, axis=-1, keepdims=True))

def reference(fields, conv_kernel, layer_norm_gain, qkv_weight, out_weight, score_bias, pattern, cotangent):
    scale_everywhere = 1.0 / math.sqrt(TOKENS)
    head_scale = HEAD_DIM ** (-0.5)
    group_count = CELLS_DEV // GROUP
    fields_f = fields.astype(jnp.float32)
    padded_fields = spread(fields_f)
    state_h = (fields_f + apply_taps(padded_fields, conv_kernel, LATS, LONS)).astype(jnp.bfloat16)
    state_f = state_h.astype(jnp.float32)
    mean_h = lax.optimization_barrier(jnp.mean(state_f, axis=-1, keepdims=True))
    mean_removed = state_f - mean_h
    var_h = lax.optimization_barrier(jnp.mean(mean_removed * mean_removed, axis=-1, keepdims=True))
    inverse_deviation = lax.rsqrt(var_h + epsilon)
    standardized_input = mean_removed * inverse_deviation
    normalized_fields = (standardized_input * layer_norm_gain).astype(jnp.bfloat16)
    inverse = jnp.argsort(pattern, axis=-1).astype(jnp.int32)
    normed_grouped = to_owner(normalized_fields, pattern)
    cot_grouped = to_owner(cotangent, pattern)

    def owner_step(carry, inputs):
        normed_g, cot_g = inputs
        qkv_rows = jnp.dot(normed_g, qkv_weight, preferred_element_type=jnp.float32).astype(jnp.bfloat16)
        split_rows = qkv_rows.reshape(group_count, GROUP, 3, HEADS, HEAD_DIM)
        queries = split_rows[:, :, 0]
        key_rows = split_rows[:, :, 1]
        value_rows = split_rows[:, :, 2]
        probs = attention_probs(queries, key_rows, score_bias)
        probs_low = probs.astype(jnp.bfloat16)
        attended = jnp.einsum('ghij,gjhd->gihd', probs_low.astype(jnp.float32), value_rows.astype(jnp.float32))
        attended = attended.astype(jnp.bfloat16).reshape(CELLS_DEV, D)
        mixed = jnp.dot(attended, out_weight, preferred_element_type=jnp.float32).astype(jnp.bfloat16)
        term = jnp.dot(attended.T, cot_g, preferred_element_type=jnp.float32)
        grad_att = jnp.dot(cot_g, out_weight.T, preferred_element_type=jnp.float32).astype(jnp.bfloat16)
        grad_heads = grad_att.reshape(group_count, GROUP, HEADS, HEAD_DIM).astype(jnp.float32)
        grad_probs = jnp.einsum('gihd,gjhd->ghij', grad_heads, value_rows.astype(jnp.float32))
        grad_scores = probs * (grad_probs - lax.optimization_barrier(jnp.sum(probs * grad_probs, axis=-1, keepdims=True)))
        grad_scores = grad_scores.astype(jnp.bfloat16).astype(jnp.float32)
        grad_query = jnp.einsum('ghij,gjhd->gihd', grad_scores, key_rows.astype(jnp.float32)) * head_scale
        grad_key = jnp.einsum('ghij,gihd->gjhd', grad_scores, queries.astype(jnp.float32)) * head_scale
        grad_value = jnp.einsum('ghij,gihd->gjhd', probs_low.astype(jnp.float32), grad_heads)
        grad_qkv = jnp.stack([grad_query, grad_key, grad_value], axis=2).astype(jnp.bfloat16)
        grad_qkv = grad_qkv.reshape(CELLS_DEV, 3 * D)
        grad_normed_g = jnp.dot(grad_qkv, qkv_weight.T, preferred_element_type=jnp.float32).astype(jnp.bfloat16)
        return (carry + term, (mixed, grad_normed_g))
    term_total, (mixed_all, grad_all) = lax.scan(owner_step, jnp.zeros((D, D), jnp.float32), (normed_grouped, cot_grouped))
    grad_project = term_total * scale_everywhere
    mixed_grid = to_grid(mixed_all, inverse)
    block_out = (state_f + mixed_grid.astype(jnp.float32)).astype(jnp.bfloat16)
    normalized_gradient = to_grid(grad_all, inverse).astype(jnp.float32)
    gain_gradient = lax.optimization_barrier(jnp.sum(normalized_gradient * standardized_input, axis=(0, 1))) * scale_everywhere
    gain_scaled = normalized_gradient * layer_norm_gain
    layer_norm_gradient = inverse_deviation * (gain_scaled - lax.optimization_barrier(jnp.mean(gain_scaled, axis=-1, keepdims=True)) - standardized_input * lax.optimization_barrier(jnp.mean(gain_scaled * standardized_input, axis=-1, keepdims=True)))
    grad_h = (cotangent.astype(jnp.float32) + layer_norm_gradient).astype(jnp.bfloat16)
    grad_hf = grad_h.astype(jnp.float32)
    padded_grad = spread(grad_hf)
    grad_fields = (grad_hf + apply_taps(padded_grad, conv_kernel[::-1, ::-1], LATS, LONS)).astype(jnp.bfloat16)
    kernel_terms = []
    for lat_tap in range(3):
        for lon_tap in range(3):
            kernel_terms.append(lax.optimization_barrier(jnp.sum(padded_fields[lat_tap:lat_tap + LATS, lon_tap:lon_tap + LONS] * grad_hf, axis=(0, 1))))
    grad_kernel = jnp.stack(kernel_terms).reshape(3, 3, D) * scale_everywhere
    return (block_out, grad_fields, grad_project, grad_kernel, gain_gradient)
```

```python
import math

import jax
import jax.numpy as jnp
from jax import lax
from jax.experimental import pallas as pl
from jax.experimental.pallas import tpu as pltpu
from jax.sharding import PartitionSpec as P

HEADS = 24
HEAD_DIM = 32
GROUP = 64
PAIR = 2 * GROUP
EDGE = 8

epsilon = 1e-05
f32, bf16 = jnp.float32, jnp.bfloat16
AXES = ("lat", "lon")
NN = (((1,), (0,)), ((), ()))
NT = (((1,), (1,)), ((), ()))
TN = (((0,), (0,)), ((), ()))
VMEM = pl.BlockSpec(memory_space=pltpu.VMEM)


def dot(a, b, dims=NN):
    return lax.dot_general(a, b, dims, preferred_element_type=f32)


def call(kernel, name, out_shape, operands, scratch=(), flops=0):
    size = sum(math.prod(x.shape) * x.dtype.itemsize for x in (*operands, *out_shape))
    return pl.pallas_call(
        kernel,
        name=name,
        out_shape=list(out_shape),
        in_specs=[VMEM] * len(operands),
        out_specs=[VMEM] * len(out_shape),
        scratch_shapes=list(scratch),
        compiler_params=pltpu.CompilerParams(vmem_limit_bytes=40 * 1024 * 1024),
        cost_estimate=pl.CostEstimate(flops=flops, bytes_accessed=size, transcendentals=0),
    )(*operands)


def shape(dims, dtype):
    return jax.ShapeDtypeStruct(dims, dtype)


def by_cell(pattern_row, cells):
    cell = lax.broadcasted_iota(jnp.int32, (cells, cells), 0)
    return jnp.where(pattern_row == cell, 1.0, 0.0).astype(bf16)


def by_slot(pattern_col, cells):
    cell = lax.broadcasted_iota(jnp.int32, (cells, cells), 1)
    return jnp.where(pattern_col == cell, 1.0, 0.0).astype(bf16)


def position_by_row(cells, slots, blocks, row_dim):
    row = lax.broadcasted_iota(jnp.int32, (cells, cells), row_dim)
    position = lax.broadcasted_iota(jnp.int32, (cells, cells), 1 - row_dim)
    place = lax.rem(row, slots) * blocks + lax.div(row, slots)
    return jnp.where(place == position, 1.0, 0.0).astype(bf16)


def pack_kernel(pattern_ref, rows_ref, out_ref):
    cells = rows_ref.shape[0]
    out_ref[...] = dot(by_slot(pattern_ref[...], cells), rows_ref[...]).astype(bf16)


def fill_pad(pad, field_ref, before_ref, after_ref, left_ref, right_ref):
    rows, cols, _ = field_ref.shape
    pad[0, EDGE : EDGE + cols] = before_ref[...].astype(f32)
    pad[rows + 1, EDGE : EDGE + cols] = after_ref[...].astype(f32)
    for row in range(rows):
        pad[row + 1, EDGE : EDGE + cols] = field_ref[row].astype(f32)
    left, right = left_ref[...].astype(f32), right_ref[...].astype(f32)
    for row in range(rows + 2):
        pad[row, EDGE - 1 : EDGE] = left[row : row + 1]
        pad[row, EDGE + cols : EDGE + cols + 1] = right[row : row + 1]


def taps_row(pad, taps, row, cols, flip):
    summed = pad[row + 1, EDGE : EDGE + cols]
    for a in range(3):
        for b in range(3):
            at = 3 * (2 - a) + 2 - b if flip else 3 * a + b
            summed = summed + taps[at : at + 1] * pad[row + a, EDGE - 1 + b : EDGE - 1 + b + cols]
    return summed


def normalized(h):
    mean = jnp.mean(h, axis=-1, keepdims=True)
    centred = h - mean
    var = jnp.mean(centred * centred, axis=-1, keepdims=True)
    deviation = lax.rsqrt(var + epsilon)
    return centred * deviation, deviation


def enter_kernel(
    pattern_ref, field_ref, before_ref, after_ref, left_ref, right_ref, taps_ref, gain_ref,
    h_ref, out_ref, pad, normed,
):
    rows, cols, _ = field_ref.shape
    fill_pad(pad, field_ref, before_ref, after_ref, left_ref, right_ref)
    taps, gain = taps_ref[...], gain_ref[...]
    for row in range(rows):
        h = taps_row(pad, taps, row, cols, False).astype(bf16)
        h_ref[row * cols : (row + 1) * cols] = h
        xhat, _ = normalized(h.astype(f32))
        normed[row * cols : (row + 1) * cols] = (xhat * gain).astype(bf16)
    out_ref[...] = dot(by_slot(pattern_ref[...], rows * cols), normed[...]).astype(bf16)


def cot_kernel(slots, blocks, arrived_ref, out_weight_ref, grad_att_ref, cot_ref):
    cells = arrived_ref.shape[0]
    grouped = dot(position_by_row(cells, slots, blocks, 1), arrived_ref[...]).astype(bf16)
    grad_att_ref[...] = dot(out_weight_ref[...], grouped, NT).astype(bf16)
    cot_ref[...] = grouped.T


def low_lanes(dims):
    return lax.broadcasted_iota(jnp.int32, dims, len(dims) - 1) < GROUP


def pair_scores(left, right):
    both = dot(left, right, TN)
    return jnp.where(low_lanes((GROUP, PAIR)), both[:GROUP], both[GROUP:])


def pair_diagonal(compact):
    low = low_lanes((GROUP, PAIR))
    zero = jnp.zeros_like(compact)
    return jnp.concatenate([jnp.where(low, compact, zero), jnp.where(low, zero, compact)], axis=0)


def forward_kernel(
    slots, blocks, unroll,
    arrived_ref, qkv_weight_t_ref, out_weight_t_ref, bias_ref,
    mixed_ref, qkv_ref, probs_ref, att_ref,
):
    cells, width = arrived_ref.shape
    grouped = dot(position_by_row(cells, slots, blocks, 1), arrived_ref[...]).astype(bf16)
    step = width // 2
    for at in range(0, 3 * width, step):
        qkv_ref[at : at + step] = dot(qkv_weight_t_ref[at : at + step], grouped, NT).astype(bf16)
    scale = HEAD_DIM ** (-0.5)

    def head(e):
        at = pl.multiple_of(e * HEAD_DIM, HEAD_DIM)
        rows = pl.ds(at, HEAD_DIM)
        bias = bias_ref[e]
        for pair in range(cells // PAIR):
            lanes = slice(pair * PAIR, (pair + 1) * PAIR)
            q = qkv_ref[rows, lanes]
            k = qkv_ref[pl.ds(width + at, HEAD_DIM), lanes]
            v = qkv_ref[pl.ds(2 * width + at, HEAD_DIM), lanes]
            scores = pair_scores(k, q) * scale + bias
            lifted = jnp.exp(scores - jnp.max(scores, axis=0, keepdims=True))
            probs = lifted / jnp.sum(lifted, axis=0, keepdims=True)
            probs_ref[e, :, lanes] = probs
            att_ref[rows, lanes] = dot(v, pair_diagonal(probs).astype(bf16)).astype(bf16)

    def heads(step, carry):
        for u in range(unroll):
            head(step * unroll + u)
        return carry

    lax.fori_loop(0, HEADS // unroll, heads, 0)
    mixed = dot(out_weight_t_ref[...], att_ref[...]).astype(bf16)
    mixed_ref[...] = dot(position_by_row(cells, slots, blocks, 0), mixed, NT).astype(bf16)


def backward_kernel(
    slots, blocks, unroll,
    qkv_ref, probs_ref, grad_att_ref, qkv_weight_ref,
    out_ref, grad_qkv,
):
    cells, width = out_ref.shape
    scale = HEAD_DIM ** (-0.5)

    def head(e):
        at = pl.multiple_of(e * HEAD_DIM, HEAD_DIM)
        rows = pl.ds(at, HEAD_DIM)
        key_rows, value_rows = pl.ds(width + at, HEAD_DIM), pl.ds(2 * width + at, HEAD_DIM)
        for pair in range(cells // PAIR):
            lanes = slice(pair * PAIR, (pair + 1) * PAIR)
            q, k, v = qkv_ref[rows, lanes], qkv_ref[key_rows, lanes], qkv_ref[value_rows, lanes]
            grad = grad_att_ref[rows, lanes]
            probs = probs_ref[e, :, lanes]
            grad_probs = pair_scores(v, grad)
            dropped = jnp.sum(probs * grad_probs, axis=0, keepdims=True)
            grad_scores = pair_diagonal(probs * (grad_probs - dropped)).astype(bf16)
            grad_qkv[rows, lanes] = (dot(k, grad_scores) * scale).astype(bf16)
            grad_qkv[key_rows, lanes] = (dot(q, grad_scores, NT) * scale).astype(bf16)
            grad_qkv[value_rows, lanes] = dot(grad, pair_diagonal(probs).astype(bf16), NT).astype(bf16)

    def heads(step, carry):
        for u in range(unroll):
            head(step * unroll + u)
        return carry

    lax.fori_loop(0, HEADS // unroll, heads, 0)
    grad = dot(qkv_weight_ref[...], grad_qkv[...]).astype(bf16)
    out_ref[...] = dot(position_by_row(cells, slots, blocks, 0), grad, NT).astype(bf16)


def project_kernel(cot_ref, att_ref, out_ref):
    if out_ref.ndim == 2:
        out_ref[...] = dot(cot_ref[...], att_ref[...], NT).astype(bf16)
        return
    lats, lons, cols, rows = out_ref.shape
    for a in range(lats):
        part = dot(cot_ref[...], att_ref[a * rows : (a + 1) * rows], NT).astype(bf16)
        for b in range(lons):
            out_ref[a, b] = part[b * cols : (b + 1) * cols]


def leave_kernel(pattern_ref, mixed_ref, h_ref, out_ref):
    mixed = dot(by_cell(pattern_ref[...], h_ref.shape[0]), mixed_ref[...])
    out_ref[...] = (h_ref[...].astype(f32) + mixed).astype(bf16)


def return_kernel(
    pattern_ref, arrived_ref, h_ref, cot_ref, gain_ref,
    field_ref, before_ref, after_ref, left_ref, right_ref,
    grad_ref, sums_ref, pad, normed_grad,
):
    rows, cols, width = field_ref.shape
    fill_pad(pad, field_ref, before_ref, after_ref, left_ref, right_ref)
    normed_grad[...] = dot(by_cell(pattern_ref[...], rows * cols), arrived_ref[...])
    gain = gain_ref[...]

    def fold(x):
        return jnp.sum(x.reshape(cols // 8, 8, width), axis=0)

    sums = [jnp.zeros((8, width), f32) for _ in range(10)]
    for row in range(rows):
        at = slice(row * cols, (row + 1) * cols)
        xhat, deviation = normalized(h_ref[at].astype(f32))
        grad = normed_grad[at]
        sums[9] = sums[9] + fold(grad * xhat)
        u = grad * gain
        inner = u - jnp.mean(u, axis=-1, keepdims=True)
        inner = inner - xhat * jnp.mean(u * xhat, axis=-1, keepdims=True)
        grad_h = (cot_ref[at].astype(f32) + deviation * inner).astype(bf16)
        grad_ref[row] = grad_h
        grad_h = grad_h.astype(f32)
        for a in range(3):
            for b in range(3):
                moved = pad[row + a, EDGE - 1 + b : EDGE - 1 + b + cols]
                sums[3 * a + b] = sums[3 * a + b] + fold(moved * grad_h)
    for i in range(10):
        sums_ref[i : i + 1] = jnp.sum(sums[i], axis=0, keepdims=True)
    sums_ref[10:16] = jnp.zeros((6, width), f32)


def spread_kernel(
    field_ref, before_ref, after_ref, left_ref, right_ref, taps_ref, out_ref, pad
):
    rows, cols, _ = field_ref.shape
    fill_pad(pad, field_ref, before_ref, after_ref, left_ref, right_ref)
    taps = taps_ref[...]
    for row in range(rows):
        out_ref[row] = taps_row(pad, taps, row, cols, True).astype(bf16)


def swap_pairs(size, bit):
    return [(i, i ^ bit) for i in range(size)]


def rims(field):
    lat_count, lon_count = lax.axis_size("lat"), lax.axis_size("lon")
    first, last = field[0], field[-1]
    if lat_count == 2:
        low = lax.axis_index("lat") == 0
        met = lax.ppermute(jnp.where(low, last, first), "lat", [(0, 1), (1, 0)])
        none = jnp.zeros_like(met)
        before, after = jnp.where(low, none, met), jnp.where(low, met, none)
    else:
        up = [(i, i + 1) for i in range(lat_count - 1)]
        before = lax.ppermute(last, "lat", up)
        after = lax.ppermute(first, "lat", [(j, i) for i, j in up])
    right = [(i, (i + 1) % lon_count) for i in range(lon_count)]

    def column(at):
        return jnp.concatenate([before[at : at + 1], field[:, at], after[at : at + 1]], axis=0)

    from_left = lax.ppermute(column(field.shape[1] - 1), "lon", right)
    from_right = lax.ppermute(column(0), "lon", [(j, i) for i, j in right])
    return before, after, from_left, from_right


def exchange(rows):
    blocks = lax.axis_size("lat") * lax.axis_size("lon")
    cells, width = rows.shape
    sent = rows.reshape(blocks, cells // blocks, width)
    return lax.all_to_all(sent, AXES, split_axis=0, concat_axis=0, tiled=True).reshape(cells, width)


def total_over_devices(x):
    for axis in ("lon", "lat"):
        size = lax.axis_size(axis)
        if size & (size - 1):
            x = lax.psum(x, axis)
            continue
        bit = 1
        while bit < size:
            x = x + lax.ppermute(x, axis, swap_pairs(size, bit))
            bit *= 2
    return x


def body(
    fields, conv_kernel, layer_norm_gain, qkv_weight, out_weight, score_bias, pattern, cotangent
):
    rows, cols, width = fields.shape
    cells = rows * cols
    lat_count, lon_count = lax.axis_size("lat"), lax.axis_size("lon")
    blocks = lat_count * lon_count
    slots = cells // blocks
    scale_everywhere = 1.0 / math.sqrt(cells * blocks)
    pattern_row = pattern.reshape(1, cells)
    pattern_col = pattern.reshape(cells, 1)
    gain = layer_norm_gain.reshape(1, width)
    taps = conv_kernel.reshape(9, width)
    cot_rows = cotangent.reshape(cells, width)
    qkv_weight_t = qkv_weight.T
    out_weight_t = out_weight.T
    bias = jnp.swapaxes(score_bias, 1, 2)
    bias = jnp.concatenate([bias, bias], axis=2)
    pad = pltpu.VMEM((rows + 2, cols + 2 * EDGE, width), f32)
    rows_shape = shape((cells, width), bf16)
    cols_shape = shape((width, cells), bf16)
    tall_shape = shape((3 * width, cells), bf16)

    cot_packed = call(pack_kernel, "pack_cotangent", [rows_shape], [pattern_col, cot_rows])[0]
    cot_arrived = exchange(cot_packed)
    grad_att, cot_cols = call(
        lambda *refs: cot_kernel(slots, blocks, *refs),
        "cotangent_products", [cols_shape, cols_shape], [cot_arrived, out_weight],
    )

    beside = rims(fields)
    h, packed = call(
        enter_kernel, "convolve_normalize_pack", [rows_shape, rows_shape],
        [pattern_col, fields, *beside, taps, gain],
        [pad, pltpu.VMEM((cells, width), bf16)],
    )
    arrived = exchange(packed)
    mixed, qkv, probs, att = call(
        lambda *refs: forward_kernel(slots, blocks, 2, *refs),
        "attention_forward",
        [rows_shape, tall_shape, shape((HEADS, GROUP, cells), f32), cols_shape],
        [arrived, qkv_weight_t, out_weight_t, bias],
        flops=5_000_000_000,
    )
    mixed_home = exchange(mixed)
    grad_grouped = call(
        lambda *refs: backward_kernel(slots, blocks, 2, *refs),
        "attention_backward", [rows_shape], [qkv, probs, grad_att, qkv_weight],
        [pltpu.VMEM((3 * width, cells), bf16)],
        flops=10_000_000_000,
    )[0]
    grad_home = exchange(grad_grouped)

    part_rows, part_cols = width // lat_count, width // lon_count
    parts = (lat_count, lon_count, part_cols, part_rows)
    if part_rows % 128 == 0 and part_cols % 16 == 0:
        project = call(project_kernel, "project_gradient", [shape(parts, bf16)], [cot_cols, att])[0]
    else:
        project = call(project_kernel, "project_gradient", [shape((width, width), bf16)], [cot_cols, att])[0]
        project = project.reshape(lon_count, part_cols, lat_count, part_rows).transpose(2, 0, 1, 3)
    project = project.reshape(blocks, part_cols, part_rows)
    project = lax.all_to_all(project, AXES, split_axis=0, concat_axis=0, tiled=True)
    grad_project = jnp.sum(project.astype(f32), axis=0).T * scale_everywhere

    block_out = call(leave_kernel, "block_out", [rows_shape], [pattern_row, mixed_home, h])[0]
    grad_h, sums = call(
        return_kernel, "normalize_back",
        [shape(fields.shape, bf16), shape((16, width), f32)],
        [pattern_row, grad_home, h, cot_rows, gain, fields, *beside],
        [pad, pltpu.VMEM((cells, width), f32)],
    )
    grad_fields = call(
        spread_kernel, "convolve_back", [shape(fields.shape, bf16)],
        [grad_h, *rims(grad_h), taps], [pad],
    )[0]
    sums = total_over_devices(sums) * scale_everywhere
    return (
        block_out.reshape(rows, cols, width),
        grad_fields,
        grad_project,
        sums[:9].reshape(3, 3, width),
        sums[9],
    )


def solution(mesh):
    placed = (
        P("lat", "lon", None),
        P(),
        P(),
        P(),
        P(),
        P(),
        P("lat", "lon", None),
        P("lat", "lon", None),
    )
    return jax.shard_map(
        body,
        mesh=mesh,
        in_specs=placed,
        out_specs=(P("lat", "lon", None), P("lat", "lon", None), P("lat", "lon"), P(), P()),
        check_vma=False,
    )
```

```python
import math

import jax
import jax.numpy as jnp
from jax import lax
from jax.experimental import pallas as pl
from jax.experimental.pallas import tpu as pltpu
from jax.sharding import PartitionSpec as P

HEADS = 24
HEAD_DIM = 32
GROUP = 64
PAIR = 2 * GROUP
EDGE = 8
UNROLL_F = 4
UNROLL_B = 4

epsilon = 1e-05
f32, bf16 = jnp.float32, jnp.bfloat16
AXES = ("lat", "lon")
NN = (((1,), (0,)), ((), ()))
NT = (((1,), (1,)), ((), ()))
TN = (((0,), (0,)), ((), ()))
VMEM = pl.BlockSpec(memory_space=pltpu.VMEM)
SMEM = pl.BlockSpec(memory_space=pltpu.SMEM)
ANY = pl.BlockSpec(memory_space=pl.ANY)


def dot(a, b, dims=NN):
    return lax.dot_general(a, b, dims, preferred_element_type=f32)


def whole(x):
    return pl.BlockSpec(x.shape, lambda step: (0,) * len(x.shape))


def call(kernel, name, out_shape, operands, scratch=(), flops=0, specs=()):
    size = sum(math.prod(x.shape) * x.dtype.itemsize for x in (*operands, *out_shape))
    specs = dict(specs)
    return pl.pallas_call(
        kernel,
        name=name,
        grid=(1,),
        out_shape=list(out_shape),
        in_specs=[specs.get(i, whole(x)) for i, x in enumerate(operands)],
        out_specs=[whole(x) for x in out_shape],
        scratch_shapes=list(scratch),
        compiler_params=pltpu.CompilerParams(vmem_limit_bytes=40 * 1024 * 1024),
        cost_estimate=pl.CostEstimate(flops=flops, bytes_accessed=size, transcendentals=0),
    )(*operands)


def shape(dims, dtype):
    return jax.ShapeDtypeStruct(dims, dtype)


def by_cell(pattern_row, cells):
    cell = lax.broadcasted_iota(jnp.int32, (cells, cells), 0)
    return jnp.where(pattern_row == cell, 1.0, 0.0).astype(bf16)


def position_by_row(cells, slots, blocks, row_dim):
    row = lax.broadcasted_iota(jnp.int32, (cells, cells), row_dim)
    position = lax.broadcasted_iota(jnp.int32, (cells, cells), 1 - row_dim)
    place = lax.rem(row, slots) * blocks + lax.div(row, slots)
    return jnp.where(place == position, 1.0, 0.0).astype(bf16)


def pack_kernel(pattern_ref, rows_ref, out_ref):
    cells = rows_ref.shape[0]
    out_ref[...] = dot(by_cell(pattern_ref[...], cells), rows_ref[...], TN).astype(bf16)


def fill_pad(pad, field_ref, before_ref, after_ref, left_ref, right_ref):
    rows, cols, _ = field_ref.shape
    pad[0, EDGE : EDGE + cols] = before_ref[...].astype(f32)
    pad[rows + 1, EDGE : EDGE + cols] = after_ref[...].astype(f32)
    for row in range(rows):
        pad[row + 1, EDGE : EDGE + cols] = field_ref[row].astype(f32)
    left, right = left_ref[...].astype(f32), right_ref[...].astype(f32)
    for row in range(rows + 2):
        pad[row, EDGE - 1 : EDGE] = left[row : row + 1]
        pad[row, EDGE + cols : EDGE + cols + 1] = right[row : row + 1]


def taps_row(pad, taps, row, cols, flip):
    summed = pad[row + 1, EDGE : EDGE + cols]
    for a in range(3):
        for b in range(3):
            tap = taps[2 - a, 2 - b : 3 - b] if flip else taps[a, b : b + 1]
            summed = summed + tap * pad[row + a, EDGE - 1 + b : EDGE - 1 + b + cols]
    return summed


def normalized(h):
    mean = jnp.mean(h, axis=-1, keepdims=True)
    centred = h - mean
    var = jnp.mean(centred * centred, axis=-1, keepdims=True)
    deviation = lax.rsqrt(var + epsilon)
    return centred * deviation, deviation


def enter_kernel(
    pattern_ref, field_ref, before_ref, after_ref, left_ref, right_ref, taps_ref, gain_ref,
    h_ref, out_ref, pad, normed,
):
    rows, cols, _ = field_ref.shape
    fill_pad(pad, field_ref, before_ref, after_ref, left_ref, right_ref)
    taps, gain = taps_ref[...], gain_ref[...]
    for row in range(rows):
        h = taps_row(pad, taps, row, cols, False).astype(bf16)
        h_ref[row * cols : (row + 1) * cols] = h
        xhat, _ = normalized(h.astype(f32))
        normed[row * cols : (row + 1) * cols] = (xhat * gain).astype(bf16)
    out_ref[...] = dot(by_cell(pattern_ref[...], rows * cols), normed[...], TN).astype(bf16)


def cot_kernel(slots, blocks, arrived_ref, out_weight_ref, grad_att_ref, cot_ref):
    cells = arrived_ref.shape[0]
    grouped = dot(position_by_row(cells, slots, blocks, 1), arrived_ref[...]).astype(bf16)
    grad_att_ref[...] = dot(out_weight_ref[...], grouped, NT).astype(bf16)
    cot_ref[...] = grouped.T


def low_lanes(dims):
    return lax.broadcasted_iota(jnp.int32, dims, len(dims) - 1) < GROUP


def pair_scores(left, right):
    both = dot(left, right, TN)
    return jnp.where(low_lanes((GROUP, PAIR)), both[:GROUP], both[GROUP:])


def pair_diagonal(compact):
    low = low_lanes((GROUP, PAIR))
    zero = jnp.zeros_like(compact)
    return jnp.concatenate([jnp.where(low, compact, zero), jnp.where(low, zero, compact)], axis=0)


def forward_kernel(
    slots, blocks, unroll,
    arrived_ref, qkv_weight_t_ref, out_weight_t_ref, bias_ref,
    mixed_ref, qkv_ref, probs_ref, att_ref, weight, sems,
):
    cells, width = arrived_ref.shape
    step = width // 2
    copies = [
        pltpu.make_async_copy(
            qkv_weight_t_ref.at[at : at + step], weight.at[at : at + step], sems.at[at // step]
        )
        for at in range(0, 3 * width, step)
    ]
    for copy in copies:
        copy.start()
    grouped = dot(position_by_row(cells, slots, blocks, 1), arrived_ref[...]).astype(bf16)
    for at, copy in zip(range(0, 3 * width, step), copies):
        copy.wait()
        qkv_ref[at : at + step] = dot(weight[at : at + step], grouped, NT).astype(bf16)
    scale = HEAD_DIM ** (-0.5)

    def heads(step, carry):
        some = [
            (step * unroll + u, slice(pair * PAIR, (pair + 1) * PAIR))
            for u in range(unroll)
            for pair in range(cells // PAIR)
        ]

        def rows(part, e):
            return pl.ds(pl.multiple_of(part * width + e * HEAD_DIM, HEAD_DIM), HEAD_DIM)

        scores = [
            pair_scores(qkv_ref[rows(1, e), at], qkv_ref[rows(0, e), at]) * scale + bias_ref[e]
            for e, at in some
        ]
        lifted = [jnp.exp(x - jnp.max(x, axis=0, keepdims=True)) for x in scores]
        probs = [x / jnp.sum(x, axis=0, keepdims=True) for x in lifted]
        att = [
            dot(qkv_ref[rows(2, e), at], pair_diagonal(x).astype(bf16))
            for (e, at), x in zip(some, probs)
        ]
        for (e, at), x, y in zip(some, probs, att):
            probs_ref[e, :, at] = x
            att_ref[rows(0, e), at] = y.astype(bf16)
        return carry

    lax.fori_loop(0, HEADS // unroll, heads, 0)
    mixed = dot(out_weight_t_ref[...], att_ref[...]).astype(bf16)
    mixed_ref[...] = dot(position_by_row(cells, slots, blocks, 0), mixed, NT).astype(bf16)


def backward_kernel(
    slots, blocks, unroll,
    qkv_ref, probs_ref, grad_att_ref, qkv_weight_ref,
    out_ref, grad_qkv,
):
    cells, width = out_ref.shape
    scale = HEAD_DIM ** (-0.5)

    def heads(step, carry):
        some = [
            (step * unroll + u, slice(pair * PAIR, (pair + 1) * PAIR))
            for u in range(unroll)
            for pair in range(cells // PAIR)
        ]

        def rows(part, e):
            return pl.ds(pl.multiple_of(part * width + e * HEAD_DIM, HEAD_DIM), HEAD_DIM)

        grads = [grad_att_ref[rows(0, e), at] for e, at in some]
        probs = [probs_ref[e, :, at] for e, at in some]
        grad_probs = [
            pair_scores(qkv_ref[rows(2, e), at], grad) for (e, at), grad in zip(some, grads)
        ]
        to_value = [
            dot(grad, pair_diagonal(x).astype(bf16), NT) for grad, x in zip(grads, probs)
        ]
        grad_scores = []
        for x, y in zip(probs, grad_probs):
            product = x * y
            z = product - x * jnp.sum(product, axis=0, keepdims=True)
            grad_scores.append(pair_diagonal(z).astype(bf16))
        to_query = [
            dot(qkv_ref[rows(1, e), at], x) * scale for (e, at), x in zip(some, grad_scores)
        ]
        to_key = [
            dot(qkv_ref[rows(0, e), at], x, NT) * scale for (e, at), x in zip(some, grad_scores)
        ]
        for (e, at), x, y, z in zip(some, to_query, to_key, to_value):
            grad_qkv[rows(0, e), at] = x.astype(bf16)
            grad_qkv[rows(1, e), at] = y.astype(bf16)
            grad_qkv[rows(2, e), at] = z.astype(bf16)
        return carry

    lax.fori_loop(0, HEADS // unroll, heads, 0)
    grad = dot(qkv_weight_ref[...], grad_qkv[...]).astype(bf16)
    out_ref[...] = dot(position_by_row(cells, slots, blocks, 0), grad, NT).astype(bf16)


def project_kernel(cot_ref, att_ref, out_ref):
    out_ref[...] = dot(cot_ref[...], att_ref[...], NT).astype(bf16)


def project_halves_kernel(core_ref, cot_ref, att_ref, kept_ref, sent_ref, part):
    lats, chips, cols, rows = kept_ref.shape
    core = core_ref[0]
    for a in range(lats):
        part[...] = dot(cot_ref[...], att_ref[a * rows : (a + 1) * rows], NT).astype(bf16)
        for chip in range(chips):
            kept_ref[a, chip] = part[pl.ds(pl.multiple_of((2 * chip + core) * cols, 16), cols)]
            sent_ref[a, chip] = part[pl.ds(pl.multiple_of((2 * chip + 1 - core) * cols, 16), cols)]


def join_halves_kernel(lat_ref, kept_ref, met_ref, out_ref, sent_ref):
    lat = lat_ref[0]
    out_ref[...] = (kept_ref[lat].astype(f32) + met_ref[lat].astype(f32)).astype(bf16)
    sent_ref[...] = (kept_ref[1 - lat].astype(f32) + met_ref[1 - lat].astype(f32)).astype(bf16)


def leave_kernel(pattern_ref, mixed_ref, h_ref, out_ref):
    mixed = dot(by_cell(pattern_ref[...], h_ref.shape[0]), mixed_ref[...])
    out_ref[...] = (h_ref[...].astype(f32) + mixed).astype(bf16)


def return_kernel(
    lat_ref, pattern_ref, arrived_ref, h_ref, cot_ref, gain_ref,
    field_ref, before_ref, after_ref, left_ref, right_ref,
    grad_ref, sums_ref, message_ref, pad, normed_grad,
):
    rows, cols, width = field_ref.shape
    fill_pad(pad, field_ref, before_ref, after_ref, left_ref, right_ref)
    normed_grad[...] = dot(by_cell(pattern_ref[...], rows * cols), arrived_ref[...])
    gain = gain_ref[...]

    def fold(x):
        return jnp.sum(x.reshape(cols // 8, 8, width), axis=0)

    sums = [jnp.zeros((8, width), f32) for _ in range(10)]
    for row in range(rows):
        at = slice(row * cols, (row + 1) * cols)
        xhat, deviation = normalized(h_ref[at].astype(f32))
        grad = normed_grad[at]
        sums[9] = sums[9] + fold(grad * xhat)
        u = grad * gain
        inner = u - jnp.mean(u, axis=-1, keepdims=True)
        inner = inner - xhat * jnp.mean(u * xhat, axis=-1, keepdims=True)
        grad_h = (cot_ref[at].astype(f32) + deviation * inner).astype(bf16)
        grad_ref[row] = grad_h
        grad_h = grad_h.astype(f32)
        for a in range(3):
            for b in range(3):
                moved = pad[row + a, EDGE - 1 + b : EDGE - 1 + b + cols]
                sums[3 * a + b] = sums[3 * a + b] + fold(moved * grad_h)
    for i in range(10):
        sums_ref[i : i + 1] = jnp.sum(sums[i], axis=0, keepdims=True)
    sums_ref[10:16] = jnp.zeros((6, width), f32)
    low = lat_ref[0] == 0
    message_ref[:cols] = jnp.where(low, grad_ref[rows - 1], grad_ref[0])
    total = sums_ref[...]
    high = total.astype(bf16)
    message_ref[cols : cols + 16] = high
    message_ref[cols + 16 :] = (total - high.astype(f32)).astype(bf16)


def spread_kernel(
    field_ref, before_ref, after_ref, left_ref, right_ref, taps_ref, out_ref, pad
):
    rows, cols, _ = field_ref.shape
    fill_pad(pad, field_ref, before_ref, after_ref, left_ref, right_ref)
    taps = taps_ref[...]
    for row in range(rows):
        out_ref[row] = taps_row(pad, taps, row, cols, True).astype(bf16)


def swap_pairs(size, bit):
    return [(i, i ^ bit) for i in range(size)]


def rims(field, met=None):
    lat_count, lon_count = lax.axis_size("lat"), lax.axis_size("lon")
    first, last = field[0], field[-1]
    if lat_count == 2:
        low = lax.axis_index("lat") == 0
        if met is None:
            met = lax.ppermute(jnp.where(low, last, first), "lat", swap_pairs(2, 1))
        none = jnp.zeros_like(met)
        before, after = jnp.where(low, none, met), jnp.where(low, met, none)
    else:
        up = [(i, i + 1) for i in range(lat_count - 1)]
        before = lax.ppermute(last, "lat", up)
        after = lax.ppermute(first, "lat", [(j, i) for i, j in up])
    right = [(i, (i + 1) % lon_count) for i in range(lon_count)]

    def column(at):
        return jnp.concatenate([before[at : at + 1], field[:, at], after[at : at + 1]], axis=0)

    from_left = lax.ppermute(column(field.shape[1] - 1), "lon", right)
    from_right = lax.ppermute(column(0), "lon", [(j, i) for i, j in right])
    return before, after, from_left, from_right


def exchange(rows):
    blocks = lax.axis_size("lat") * lax.axis_size("lon")
    cells, width = rows.shape
    sent = rows.reshape(blocks, cells // blocks, width)
    return lax.all_to_all(sent, AXES, split_axis=0, concat_axis=0, tiled=True).reshape(cells, width)


def scattered_project(cot_cols, att):
    width = att.shape[0]
    lat_count, lon_count = lax.axis_size("lat"), lax.axis_size("lon")
    rows, cols = width // lat_count, width // lon_count
    if lat_count != 2 or lon_count % 2 or rows % 128 or cols % 16:
        parts = call(project_kernel, "project_gradient", [shape((width, width), bf16)], [cot_cols, att])[0]
        parts = parts.reshape(lon_count, cols, lat_count, rows).transpose(2, 0, 1, 3)
        parts = parts.reshape(lat_count * lon_count, cols, rows)
        parts = lax.all_to_all(parts, AXES, split_axis=0, concat_axis=0, tiled=True)
        return jnp.sum(parts.astype(f32), axis=0).T
    chips = lon_count // 2
    lat, lon = lax.axis_index("lat").reshape(1), lax.axis_index("lon").reshape(1)
    halves = shape((lat_count, chips, cols, rows), bf16)
    quarters = shape((chips, cols, rows), bf16)
    kept, sent = call(
        project_halves_kernel, "project_gradient", [halves, halves],
        [lax.rem(lon, 2), cot_cols, att], [pltpu.VMEM((width, rows), bf16)], specs={0: SMEM},
    )
    met = lax.ppermute(sent, "lon", swap_pairs(lon_count, 1))
    kept, sent = call(
        join_halves_kernel, "project_join", [quarters, quarters], [lat, kept, met], specs={0: SMEM}
    )
    met = lax.ppermute(sent, "lat", swap_pairs(2, 1))
    parts = (kept.astype(f32) + met.astype(f32)).astype(bf16)
    groups = [[2 * chip + core for chip in range(chips)] for core in range(2)]
    parts = lax.all_to_all(
        parts, "lon", split_axis=0, concat_axis=0, axis_index_groups=groups, tiled=True
    )
    return jnp.sum(parts.astype(f32), axis=0).T


def total_over(axis, x, first=1, end=None):
    size = lax.axis_size(axis)
    if size & (size - 1):
        return lax.psum(x, axis) if end is None else x
    bit = first
    while bit < (end or size):
        x = x + lax.ppermute(x, axis, swap_pairs(size, bit))
        bit *= 2
    return x


def body(
    fields, conv_kernel, layer_norm_gain, qkv_weight, out_weight, score_bias, pattern, cotangent
):
    rows, cols, width = fields.shape
    cells = rows * cols
    lat_count, lon_count = lax.axis_size("lat"), lax.axis_size("lon")
    blocks = lat_count * lon_count
    slots = cells // blocks
    scale_everywhere = 1.0 / math.sqrt(cells * blocks)
    pattern_row = pattern.reshape(1, cells)
    gain = layer_norm_gain.reshape(1, width)
    cot_rows = cotangent.reshape(cells, width)
    qkv_weight_t = qkv_weight.T
    out_weight_t = out_weight.T
    bias = jnp.swapaxes(score_bias, 1, 2)
    bias = jnp.concatenate([bias, bias], axis=2)
    pad = pltpu.VMEM((rows + 2, cols + 2 * EDGE, width), f32)
    rows_shape = shape((cells, width), bf16)
    cols_shape = shape((width, cells), bf16)
    tall_shape = shape((3 * width, cells), bf16)

    cot_packed = call(pack_kernel, "pack_cotangent", [rows_shape], [pattern_row, cot_rows])[0]
    cot_arrived = exchange(cot_packed)
    grad_att, cot_cols = call(
        lambda *refs: cot_kernel(slots, blocks, *refs),
        "cotangent_products", [cols_shape, cols_shape], [cot_arrived, out_weight],
    )

    beside = rims(fields)
    h, packed = call(
        enter_kernel, "convolve_normalize_pack", [rows_shape, rows_shape],
        [pattern_row, fields, *beside, conv_kernel, gain],
        [pad, pltpu.VMEM((cells, width), bf16)],
    )
    arrived = exchange(packed)
    mixed, qkv, probs, att = call(
        lambda *refs: forward_kernel(slots, blocks, UNROLL_F, *refs),
        "attention_forward",
        [rows_shape, tall_shape, shape((HEADS, GROUP, cells), f32), cols_shape],
        [arrived, qkv_weight_t, out_weight_t, bias],
        [pltpu.VMEM((3 * width, width), bf16), pltpu.SemaphoreType.DMA((6,))],
        flops=5_000_000_000,
        specs={1: ANY},
    )
    grad_grouped = call(
        lambda *refs: backward_kernel(slots, blocks, UNROLL_B, *refs),
        "attention_backward", [rows_shape], [qkv, probs, grad_att, qkv_weight],
        [pltpu.VMEM((3 * width, cells), bf16)],
        flops=10_000_000_000,
    )[0]
    grad_home = exchange(grad_grouped)
    grad_home, mixed = lax.optimization_barrier((grad_home, mixed))
    mixed_home = exchange(mixed)

    grad_project = scattered_project(cot_cols, att) * scale_everywhere

    block_out = call(leave_kernel, "block_out", [rows_shape], [pattern_row, mixed_home, h])[0]
    grad_h, sums, message = call(
        return_kernel, "normalize_back",
        [shape(fields.shape, bf16), shape((16, width), f32), shape((cols + 32, width), bf16)],
        [
            lax.axis_index("lat").reshape(1), pattern_row, grad_home, h, cot_rows, gain,
            fields, *beside,
        ],
        [pad, pltpu.VMEM((cells, width), f32)], specs={0: SMEM},
    )
    if lat_count == 2:
        met = lax.ppermute(message, "lat", swap_pairs(2, 1))
        sums = sums + met[cols : cols + 16].astype(f32) + met[cols + 16 :].astype(f32)
        beside = rims(grad_h, met[:cols])
    else:
        sums = total_over("lat", sums)
        beside = rims(grad_h)
    sums = total_over("lon", sums, 1, 4)
    sums, *beside = lax.optimization_barrier((sums, *beside))
    sums = total_over("lon", sums, 4) * scale_everywhere
    grad_fields = call(
        spread_kernel, "convolve_back", [shape(fields.shape, bf16)],
        [grad_h, *beside, conv_kernel], [pad],
    )[0]
    return (
        block_out.reshape(rows, cols, width),
        grad_fields,
        grad_project,
        sums[:9].reshape(3, 3, width),
        sums[9],
    )


def solution(mesh):
    placed = (
        P("lat", "lon", None),
        P(),
        P(),
        P(),
        P(),
        P(),
        P("lat", "lon", None),
        P("lat", "lon", None),
    )
    return jax.shard_map(
        body,
        mesh=mesh,
        in_specs=placed,
        out_specs=(P("lat", "lon", None), P("lat", "lon", None), P("lat", "lon"), P(), P()),
        check_vma=False,
    )
```

```python
import math

import jax
import jax.numpy as jnp
from jax import lax
from jax.experimental import pallas as pl
from jax.experimental.pallas import tpu as pltpu
from jax.sharding import PartitionSpec as P

HEADS = 24
HEAD_DIM = 32
GROUP = 64
PAIR = 2 * GROUP
EDGE = 8
UNROLL = 6

epsilon = 1e-05
f32, bf16 = jnp.float32, jnp.bfloat16
AXES = ("lat", "lon")
NN = (((1,), (0,)), ((), ()))
NT = (((1,), (1,)), ((), ()))
TN = (((0,), (0,)), ((), ()))
VMEM = pl.BlockSpec(memory_space=pltpu.VMEM)
SMEM = pl.BlockSpec(memory_space=pltpu.SMEM)
ANY = pl.BlockSpec(memory_space=pl.ANY)
BIG = 60


def dot(a, b, dims=NN):
    return lax.dot_general(a, b, dims, preferred_element_type=f32)


def whole(x):
    return pl.BlockSpec(x.shape, lambda step: (0,) * len(x.shape))


def call(kernel, name, out_shape, operands, scratch=(), flops=0, specs=(), mib=40):
    size = sum(math.prod(x.shape) * x.dtype.itemsize for x in (*operands, *out_shape))
    specs = dict(specs)
    return pl.pallas_call(
        kernel,
        name=name,
        grid=(1,),
        out_shape=list(out_shape),
        in_specs=[specs.get(i, whole(x)) for i, x in enumerate(operands)],
        out_specs=[whole(x) for x in out_shape],
        scratch_shapes=list(scratch),
        compiler_params=pltpu.CompilerParams(vmem_limit_bytes=mib * 1024 * 1024),
        cost_estimate=pl.CostEstimate(flops=flops, bytes_accessed=size, transcendentals=0),
    )(*operands)


def shape(dims, dtype):
    return jax.ShapeDtypeStruct(dims, dtype)


def by_cell(pattern_row, cells):
    cell = lax.broadcasted_iota(jnp.int32, (cells, cells), 0)
    return jnp.where(pattern_row == cell, 1.0, 0.0).astype(bf16)


def position_by_row(cells, slots, blocks, row_dim):
    row = lax.broadcasted_iota(jnp.int32, (cells, cells), row_dim)
    position = lax.broadcasted_iota(jnp.int32, (cells, cells), 1 - row_dim)
    place = lax.rem(row, slots) * blocks + lax.div(row, slots)
    return jnp.where(place == position, 1.0, 0.0).astype(bf16)


def rim_cells(flags_ref, field_ref, row_ref, cols_ref):
    rows, cols, _ = field_ref.shape
    low, even = flags_ref[0] == 0, flags_ref[2] == 0
    row_ref[...] = jnp.where(low, field_ref[rows - 1], field_ref[0])
    first = jnp.concatenate([field_ref[row, 0:1] for row in range(rows)], axis=0)
    last = jnp.concatenate([field_ref[row, cols - 1 : cols] for row in range(rows)], axis=0)
    cols_ref[0] = jnp.where(even, last, first)
    cols_ref[1] = jnp.where(even, first, last)


def start_kernel(flags_ref, pattern_ref, rows_ref, field_ref, out_ref, row_ref, cols_ref):
    cells = rows_ref.shape[0]
    rim_cells(flags_ref, field_ref, row_ref, cols_ref)
    out_ref[...] = dot(by_cell(pattern_ref[...], cells), rows_ref[...], TN).astype(bf16)


def fill_pad(pad, flags_ref, field_ref, before_ref, after_ref, even_ref, odd_ref):
    rows, cols, _ = field_ref.shape
    before, after = before_ref[...].astype(f32), after_ref[...].astype(f32)
    pad[0, EDGE : EDGE + cols] = jnp.where(flags_ref[0] != 0, before, jnp.zeros_like(before))
    pad[rows + 1, EDGE : EDGE + cols] = jnp.where(flags_ref[1] != 0, after, jnp.zeros_like(after))
    for row in range(rows):
        pad[row + 1, EDGE : EDGE + cols] = field_ref[row].astype(f32)
    even, odd = even_ref[...].astype(f32), odd_ref[...].astype(f32)
    left = jnp.where(flags_ref[2] == 0, odd, even)
    right = jnp.where(flags_ref[2] == 0, even, odd)
    for row in range(rows + 2):
        pad[row, EDGE - 1 : EDGE] = left[row : row + 1]
        pad[row, EDGE + cols : EDGE + cols + 1] = right[row : row + 1]


def taps_row(pad, taps, row, cols, flip):
    summed = pad[row + 1, EDGE : EDGE + cols]
    for a in range(3):
        for b in range(3):
            tap = taps[2 - a, 2 - b : 3 - b] if flip else taps[a, b : b + 1]
            summed = summed + tap * pad[row + a, EDGE - 1 + b : EDGE - 1 + b + cols]
    return summed


def normalized(h):
    mean = jnp.mean(h, axis=-1, keepdims=True)
    centred = h - mean
    var = jnp.mean(centred * centred, axis=-1, keepdims=True)
    deviation = lax.rsqrt(var + epsilon)
    return centred * deviation, deviation


def enter_kernel(
    flags_ref, pattern_ref, field_ref, before_ref, after_ref, even_ref, odd_ref, taps_ref, gain_ref,
    h_ref, out_ref, pad, normed,
):
    rows, cols, _ = field_ref.shape
    fill_pad(pad, flags_ref, field_ref, before_ref, after_ref, even_ref, odd_ref)
    taps, gain = taps_ref[...], gain_ref[...]
    for row in range(rows):
        h = taps_row(pad, taps, row, cols, False).astype(bf16)
        h_ref[row * cols : (row + 1) * cols] = h
        xhat, _ = normalized(h.astype(f32))
        normed[row * cols : (row + 1) * cols] = (xhat * gain).astype(bf16)
    out_ref[...] = dot(by_cell(pattern_ref[...], rows * cols), normed[...], TN).astype(bf16)


def cot_kernel(slots, blocks, arrived_ref, out_weight_ref, grad_att_ref, cot_ref):
    cells = arrived_ref.shape[0]
    grouped = dot(position_by_row(cells, slots, blocks, 1), arrived_ref[...]).astype(bf16)
    grad_att_ref[...] = dot(out_weight_ref[...], grouped, NT).astype(bf16)
    cot_ref[...] = grouped.T


def low_lanes(dims):
    return lax.broadcasted_iota(jnp.int32, dims, len(dims) - 1) < GROUP


def pair_scores(left, right):
    both = dot(left, right, TN)
    return jnp.where(low_lanes((GROUP, PAIR)), both[:GROUP], both[GROUP:])


def pair_diagonal(compact):
    low = low_lanes((GROUP, PAIR))
    zero = jnp.zeros_like(compact)
    return jnp.concatenate([jnp.where(low, compact, zero), jnp.where(low, zero, compact)], axis=0)


def attention_kernel(
    slots, blocks, unroll,
    arrived_hbm, qkv_weight_t_hbm, bias_hbm, grad_att_hbm, qkv_weight_hbm,
    grad_ref, att_ref,
    arrived, qkv_weight_t, bias, grad_att, qkv_weight, qkv, grad_qkv, sems,
):
    cells, width = arrived.shape
    step = width // 2
    parts = [pl.ds(at, step) for at in range(0, 3 * width, step)]
    fetches = [
        pltpu.make_async_copy(source, target, sems.at[i])
        for i, (source, target) in enumerate(
            [
                (arrived_hbm, arrived),
                *((qkv_weight_t_hbm.at[part], qkv_weight_t.at[part]) for part in parts),
                (bias_hbm, bias),
                (grad_att_hbm, grad_att),
                (qkv_weight_hbm, qkv_weight),
            ]
        )
    ]
    for fetch in fetches:
        fetch.start()
    gather = position_by_row(cells, slots, blocks, 1)
    fetches[0].wait()
    grouped = dot(gather, arrived[...]).astype(bf16)
    for part, fetch in zip(parts, fetches[1:]):
        fetch.wait()
        qkv[part] = dot(qkv_weight_t[part], grouped, NT).astype(bf16)
    fetches[-3].wait()
    fetches[-2].wait()
    scale = HEAD_DIM ** (-0.5)

    def heads(step, carry):
        some = [
            (step * unroll + u, slice(pair * PAIR, (pair + 1) * PAIR))
            for u in range(unroll)
            for pair in range(cells // PAIR)
        ]

        def rows(part, e):
            return pl.ds(pl.multiple_of(part * width + e * HEAD_DIM, HEAD_DIM), HEAD_DIM)

        def q(e, at):
            return qkv[rows(0, e), at]

        def k(e, at):
            return qkv[rows(1, e), at]

        def v(e, at):
            return qkv[rows(2, e), at]

        def grad(e, at):
            return grad_att[rows(0, e), at]

        scores = [pair_scores(k(*x), q(*x)) * scale + bias[x[0]] for x in some]
        grad_probs = [pair_scores(v(*x), grad(*x)) for x in some]
        lifted = [jnp.exp(y - jnp.max(y, axis=0, keepdims=True)) for y in scores]
        probs = [y / jnp.sum(y, axis=0, keepdims=True) for y in lifted]
        probs_low = [pair_diagonal(y).astype(bf16) for y in probs]
        att = [dot(v(*x), y) for x, y in zip(some, probs_low)]
        to_value = [dot(grad(*x), y, NT) for x, y in zip(some, probs_low)]
        grad_scores = []
        for y, z in zip(probs, grad_probs):
            product = y * z
            inner = product - y * jnp.sum(product, axis=0, keepdims=True)
            grad_scores.append(pair_diagonal(inner).astype(bf16))
        to_query = [dot(k(*x), y) * scale for x, y in zip(some, grad_scores)]
        to_key = [dot(q(*x), y, NT) * scale for x, y in zip(some, grad_scores)]
        for i, (e, at) in enumerate(some):
            att_ref[rows(0, e), at] = att[i].astype(bf16)
            grad_qkv[rows(0, e), at] = to_query[i].astype(bf16)
            grad_qkv[rows(1, e), at] = to_key[i].astype(bf16)
            grad_qkv[rows(2, e), at] = to_value[i].astype(bf16)
        return carry

    lax.fori_loop(0, HEADS // unroll, heads, 0)
    fetches[-1].wait()
    grad = dot(qkv_weight[...], grad_qkv[...]).astype(bf16)
    grad_ref[...] = dot(position_by_row(cells, slots, blocks, 0), grad, NT).astype(bf16)


def mix(slots, blocks, out_weight_t_ref, att_ref, mixed_ref):
    mixed = dot(out_weight_t_ref[...], att_ref[...]).astype(bf16)
    scatter = position_by_row(att_ref.shape[1], slots, blocks, 0)
    mixed_ref[...] = dot(scatter, mixed, NT).astype(bf16)


def products_kernel(slots, blocks, cot_ref, att_ref, out_weight_t_ref, mixed_ref, out_ref):
    out_ref[...] = dot(cot_ref[...], att_ref[...], NT).astype(bf16)
    mix(slots, blocks, out_weight_t_ref, att_ref, mixed_ref)


def halves_kernel(
    slots, blocks, flags_ref, cot_ref, att_ref, out_weight_t_ref, mixed_ref, kept_ref, sent_ref, part
):
    lats, chips, cols, rows = kept_ref.shape
    core = flags_ref[2]
    for a in range(lats):
        part[...] = dot(cot_ref[...], att_ref[a * rows : (a + 1) * rows], NT).astype(bf16)
        for chip in range(chips):
            kept_ref[a, chip] = part[pl.ds(pl.multiple_of((2 * chip + core) * cols, 16), cols)]
            sent_ref[a, chip] = part[pl.ds(pl.multiple_of((2 * chip + 1 - core) * cols, 16), cols)]
    mix(slots, blocks, out_weight_t_ref, att_ref, mixed_ref)


def join_halves_kernel(flags_ref, kept_ref, met_ref, out_ref, sent_ref):
    lat = jnp.minimum(flags_ref[0], 1)
    out_ref[...] = (kept_ref[lat].astype(f32) + met_ref[lat].astype(f32)).astype(bf16)
    sent_ref[...] = (kept_ref[1 - lat].astype(f32) + met_ref[1 - lat].astype(f32)).astype(bf16)


def leave_kernel(pattern_ref, mixed_ref, h_ref, out_ref):
    mixed = dot(by_cell(pattern_ref[...], h_ref.shape[0]), mixed_ref[...])
    out_ref[...] = (h_ref[...].astype(f32) + mixed).astype(bf16)


def return_kernel(
    flags_ref, pattern_ref, arrived_ref, h_ref, cot_ref, gain_ref,
    field_ref, before_ref, after_ref, even_ref, odd_ref,
    grad_ref, sums_ref, message_ref, columns_ref, pad, normed_grad,
):
    rows, cols, width = field_ref.shape
    fill_pad(pad, flags_ref, field_ref, before_ref, after_ref, even_ref, odd_ref)
    normed_grad[...] = dot(by_cell(pattern_ref[...], rows * cols), arrived_ref[...])
    gain = gain_ref[...]

    def fold(x):
        return jnp.sum(x.reshape(cols // 8, 8, width), axis=0)

    sums = [jnp.zeros((8, width), f32) for _ in range(10)]
    for row in range(rows):
        at = slice(row * cols, (row + 1) * cols)
        xhat, deviation = normalized(h_ref[at].astype(f32))
        grad = normed_grad[at]
        sums[9] = sums[9] + fold(grad * xhat)
        u = grad * gain
        inner = u - jnp.mean(u, axis=-1, keepdims=True)
        inner = inner - xhat * jnp.mean(u * xhat, axis=-1, keepdims=True)
        grad_h = (cot_ref[at].astype(f32) + deviation * inner).astype(bf16)
        grad_ref[row] = grad_h
        grad_h = grad_h.astype(f32)
        for a in range(3):
            for b in range(3):
                moved = pad[row + a, EDGE - 1 + b : EDGE - 1 + b + cols]
                sums[3 * a + b] = sums[3 * a + b] + fold(moved * grad_h)
    for i in range(10):
        sums_ref[i : i + 1] = jnp.sum(sums[i], axis=0, keepdims=True)
    sums_ref[10:16] = jnp.zeros((6, width), f32)
    rim_cells(flags_ref, grad_ref, message_ref.at[:cols], columns_ref)
    total = sums_ref[...]
    high = total.astype(bf16)
    message_ref[cols : cols + 16] = high
    message_ref[cols + 16 :] = (total - high.astype(f32)).astype(bf16)


def spread_kernel(
    flags_ref, field_ref, before_ref, after_ref, even_ref, odd_ref, taps_ref, out_ref, pad
):
    rows, cols, _ = field_ref.shape
    fill_pad(pad, flags_ref, field_ref, before_ref, after_ref, even_ref, odd_ref)
    taps = taps_ref[...]
    for row in range(rows):
        out_ref[row] = taps_row(pad, taps, row, cols, True).astype(bf16)


def swap_pairs(size, bit):
    return [(i, i ^ bit) for i in range(size)]


def lat_rims(field, met):
    if lax.axis_size("lat") == 2:
        return met, met
    up = [(i, i + 1) for i in range(lax.axis_size("lat") - 1)]
    before = lax.ppermute(field[-1], "lat", up)
    after = lax.ppermute(field[0], "lat", [(j, i) for i, j in up])
    return before, after


def lon_rims(flags, rows, columns, riders=None):
    lon_count = lax.axis_size("lon")
    before, after = rows
    even = flags[2] == 0

    def column(which, last):
        at = before.shape[0] - 1

        def corner(row, there):
            cell = jnp.where(last, row[at:], row[:1])
            return jnp.where(there, cell, jnp.zeros_like(cell))

        return jnp.concatenate(
            [corner(before, flags[0] != 0), columns[which], corner(after, flags[1] != 0)], axis=0
        )

    sent = column(0, even)
    if riders is not None:
        sent = jnp.concatenate([riders, sent], axis=0)
    met_even = lax.ppermute(sent, "lon", swap_pairs(lon_count, 1))
    odd_pairs = [(i, (i + 1 if i % 2 else i - 1) % lon_count) for i in range(lon_count)]
    met_odd = lax.ppermute(column(1, jnp.logical_not(even)), "lon", odd_pairs)
    if riders is None:
        return met_even, met_odd
    count = riders.shape[0]
    return met_even[count:], met_odd, met_even[:count]


def exchange(rows):
    blocks = lax.axis_size("lat") * lax.axis_size("lon")
    cells, width = rows.shape
    sent = rows.reshape(blocks, cells // blocks, width)
    return lax.all_to_all(sent, AXES, split_axis=0, concat_axis=0, tiled=True).reshape(cells, width)


def attended_products(slots, blocks, flags, cot_cols, att, out_weight_t):
    width, cells = att.shape
    lat_count, lon_count = lax.axis_size("lat"), lax.axis_size("lon")
    rows, cols = width // lat_count, width // lon_count
    mixed_shape = shape((cells, width), bf16)
    if lat_count != 2 or lon_count % 4 or lon_count & (lon_count - 1) or rows % 128 or cols % 16:
        mixed, parts = call(
            lambda *refs: products_kernel(slots, blocks, *refs),
            "attended_products", [mixed_shape, shape((width, width), bf16)],
            [cot_cols, att, out_weight_t],
        )
        parts = parts.reshape(lon_count, cols, lat_count, rows).transpose(2, 0, 1, 3)
        parts = parts.reshape(lat_count * lon_count, cols, rows)
        parts = lax.all_to_all(parts, AXES, split_axis=0, concat_axis=0, tiled=True)
        return mixed, jnp.sum(parts.astype(f32), axis=0)
    halves = shape((lat_count, lon_count // 2, cols, rows), bf16)
    quarters = shape((lon_count // 2, cols, rows), bf16)
    mixed, kept, sent = call(
        lambda *refs: halves_kernel(slots, blocks, *refs),
        "attended_products", [mixed_shape, halves, halves],
        [flags, cot_cols, att, out_weight_t],
        [pltpu.VMEM((width, rows), bf16)], specs={0: SMEM},
    )
    met = lax.ppermute(sent, "lon", swap_pairs(lon_count, 1))
    kept, sent = call(
        join_halves_kernel, "project_join", [quarters, quarters], [flags, kept, met], specs={0: SMEM}
    )
    met = lax.ppermute(sent, "lat", swap_pairs(2, 1))
    parts = (kept.astype(f32) + met.astype(f32)).astype(bf16)
    kept, sent = halved(parts, 2)
    return mixed, (kept, lax.ppermute(sent, "lon", swap_pairs(lon_count, 2)))


def halved(parts, bit):
    mine = lax.rem(lax.div(lax.axis_index("lon"), bit), 2)
    pairs = parts.reshape(parts.shape[0] // 2, 2, *parts.shape[1:])
    kept = lax.dynamic_index_in_dim(pairs, mine, 1, keepdims=False)
    return kept, lax.dynamic_index_in_dim(pairs, 1 - mine, 1, keepdims=False)


def two_terms(x):
    high = x.astype(bf16)
    return jnp.concatenate([high, (x - high.astype(f32)).astype(bf16)], axis=0)


def one_term(x):
    half = x.shape[0] // 2
    return x[:half].astype(f32) + x[half:].astype(f32)


def total_over(axis, x):
    size, bit = lax.axis_size(axis), 1
    if size & (size - 1):
        return lax.psum(x, axis)
    while bit < size:
        x = x + lax.ppermute(x, axis, swap_pairs(size, bit))
        bit *= 2
    return x


def body(
    fields, conv_kernel, layer_norm_gain, qkv_weight, out_weight, score_bias, pattern, cotangent
):
    rows, cols, width = fields.shape
    cells = rows * cols
    lat_count, lon_count = lax.axis_size("lat"), lax.axis_size("lon")
    blocks = lat_count * lon_count
    slots = cells // blocks
    scale_everywhere = 1.0 / math.sqrt(cells * blocks)
    pattern_row = pattern.reshape(1, cells)
    gain = layer_norm_gain.reshape(1, width)
    cot_rows = cotangent.reshape(cells, width)
    qkv_weight_t = qkv_weight.T
    out_weight_t = out_weight.T
    bias = jnp.swapaxes(score_bias, 1, 2)
    bias = jnp.concatenate([bias, bias], axis=2)
    pad = pltpu.VMEM((rows + 2, cols + 2 * EDGE, width), f32)
    rows_shape = shape((cells, width), bf16)
    cols_shape = shape((width, cells), bf16)
    tall_shape = shape((3 * width, cells), bf16)

    lat, lon = lax.axis_index("lat"), lax.axis_index("lon")
    flags = jnp.stack([lat, lat_count - 1 - lat, lax.rem(lon, 2)]).astype(jnp.int32)
    row_shape, columns_shape = shape((cols, width), bf16), shape((2, rows, width), bf16)

    cot_packed, row, columns = call(
        start_kernel, "start", [rows_shape, row_shape, columns_shape],
        [flags, pattern_row, cot_rows, fields], specs={0: SMEM}, mib=BIG,
    )
    met = lax.ppermute(row, "lat", swap_pairs(2, 1)) if lat_count == 2 else None
    cot_arrived = exchange(cot_packed)
    grad_att, cot_cols = call(
        lambda *refs: cot_kernel(slots, blocks, *refs),
        "cotangent_products", [cols_shape, cols_shape], [cot_arrived, out_weight],
    )

    beside = lat_rims(fields, met)
    beside = (*beside, *lon_rims(flags, beside, columns))
    h, packed = call(
        enter_kernel, "convolve_normalize_pack", [rows_shape, rows_shape],
        [flags, pattern_row, fields, *beside, conv_kernel, gain],
        [pad, pltpu.VMEM((cells, width), bf16)], specs={0: SMEM}, mib=BIG,
    )
    arrived = exchange(packed)
    weight_shape = (width, 3 * width)
    grad_grouped, att = call(
        lambda *refs: attention_kernel(slots, blocks, UNROLL, *refs),
        "attention", [rows_shape, cols_shape],
        [arrived, qkv_weight_t, bias, grad_att, qkv_weight],
        [
            pltpu.VMEM((cells, width), bf16), pltpu.VMEM(weight_shape[::-1], bf16),
            pltpu.VMEM(bias.shape, f32), pltpu.VMEM((width, cells), bf16),
            pltpu.VMEM(weight_shape, bf16), pltpu.VMEM((3 * width, cells), bf16),
            pltpu.VMEM((3 * width, cells), bf16), pltpu.SemaphoreType.DMA((10,)),
        ],
        flops=12_000_000_000, specs=dict.fromkeys(range(5), ANY), mib=BIG,
    )
    grad_home = exchange(grad_grouped)
    mixed, project = attended_products(slots, blocks, flags, cot_cols, att, out_weight_t)
    grad_home, mixed = lax.optimization_barrier((grad_home, mixed))
    mixed_home = exchange(mixed)

    grad_h, sums, message, columns = call(
        return_kernel, "normalize_back",
        [
            shape(fields.shape, bf16), shape((16, width), f32),
            shape((cols + 32, width), bf16), columns_shape,
        ],
        [flags, pattern_row, grad_home, h, cot_rows, gain, fields, *beside],
        [pad, pltpu.VMEM((cells, width), f32)], specs={0: SMEM},
    )
    if lat_count == 2:
        met = lax.ppermute(message, "lat", swap_pairs(2, 1))
        sums = sums + one_term(met[cols:])
        beside = lat_rims(grad_h, met[:cols])
    else:
        sums = total_over("lat", sums)
        beside = lat_rims(grad_h, None)
    staged = isinstance(project, tuple)
    if staged:
        even, odd, met = lon_rims(flags, beside, columns, two_terms(sums))
        beside = (*beside, even, odd)
        sums = sums + one_term(met)
        sums = sums + lax.ppermute(sums, "lon", swap_pairs(lon_count, 2))
        sums, odd = lax.optimization_barrier((sums, odd))
        beside = (*beside[:2], even, odd)
        project = (project[0].astype(f32) + project[1].astype(f32)).astype(bf16)
        bit = 4
        while bit < lon_count:
            if 2 * bit == lon_count:
                sums, mixed_home = lax.optimization_barrier((sums, mixed_home))
            kept, sent = halved(project, bit)
            high_low = two_terms(sums).reshape(-1, sent.shape[-1])
            sent = sent.reshape(-1, sent.shape[-1])
            met = lax.ppermute(
                jnp.concatenate([high_low, sent], axis=0), "lon", swap_pairs(lon_count, bit)
            )
            sums = sums + one_term(met[: high_low.shape[0]].reshape(2 * sums.shape[0], width))
            project = kept.astype(f32) + met[high_low.shape[0] :].reshape(kept.shape).astype(f32)
            bit *= 2
            if bit < lon_count:
                project = project.astype(bf16)
        grad_project = project[0].T * scale_everywhere
    else:
        beside = (*beside, *lon_rims(flags, beside, columns))
        sums = total_over("lon", sums)
        grad_project = project.T * scale_everywhere
    sums = sums * scale_everywhere
    grad_fields = call(
        spread_kernel, "convolve_back", [shape(fields.shape, bf16)],
        [flags, grad_h, *beside, conv_kernel], [pad], specs={0: SMEM},
    )[0]
    block_out = call(leave_kernel, "block_out", [rows_shape], [pattern_row, mixed_home, h])[0]
    return (
        block_out.reshape(rows, cols, width),
        grad_fields,
        grad_project,
        sums[:9].reshape(3, 3, width),
        sums[9],
    )


def solution(mesh):
    placed = (
        P("lat", "lon", None),
        P(),
        P(),
        P(),
        P(),
        P(),
        P("lat", "lon", None),
        P("lat", "lon", None),
    )
    return jax.shard_map(
        body,
        mesh=mesh,
        in_specs=placed,
        out_specs=(P("lat", "lon", None), P("lat", "lon", None), P("lat", "lon"), P(), P()),
        check_vma=False,
    )
```

```python
import math

import jax
import jax.numpy as jnp
from jax import lax
from jax.experimental import pallas as pl
from jax.experimental.pallas import tpu as pltpu
from jax.sharding import PartitionSpec as P

HEADS = 24
HEAD_DIM = 32
GROUP = 64
PAIR = 2 * GROUP
EDGE = 8
UNROLL = 24

epsilon = 1e-05
f32, bf16 = jnp.float32, jnp.bfloat16
AXES = ("lat", "lon")
NN = (((1,), (0,)), ((), ()))
NT = (((1,), (1,)), ((), ()))
TN = (((0,), (0,)), ((), ()))
TT = (((0,), (1,)), ((), ()))
VMEM = pl.BlockSpec(memory_space=pltpu.VMEM)
SMEM = pl.BlockSpec(memory_space=pltpu.SMEM)
ANY = pl.BlockSpec(memory_space=pl.ANY)
BIG = 60


def dot(a, b, dims=NN):
    return lax.dot_general(a, b, dims, preferred_element_type=f32)


def whole(x):
    return pl.BlockSpec(x.shape, lambda step: (0,) * len(x.shape))


def call(kernel, name, out_shape, operands, scratch=(), flops=0, specs=(), mib=40):
    size = sum(math.prod(x.shape) * x.dtype.itemsize for x in (*operands, *out_shape))
    specs = dict(specs)
    return pl.pallas_call(
        kernel,
        name=name,
        grid=(1,),
        out_shape=list(out_shape),
        in_specs=[specs.get(i, whole(x)) for i, x in enumerate(operands)],
        out_specs=[whole(x) for x in out_shape],
        scratch_shapes=list(scratch),
        compiler_params=pltpu.CompilerParams(vmem_limit_bytes=mib * 1024 * 1024),
        cost_estimate=pl.CostEstimate(flops=flops, bytes_accessed=size, transcendentals=0),
    )(*operands)


def fetch(sems, *pairs):
    copies = [pltpu.make_async_copy(x, y, sems.at[i]) for i, (x, y) in enumerate(pairs)]
    for copy in copies:
        copy.start()
    return copies


def shape(dims, dtype):
    return jax.ShapeDtypeStruct(dims, dtype)


def place():
    lat, lon = lax.axis_index("lat"), lax.axis_index("lon")
    return lat, lax.axis_size("lat") - 1 - lat, lax.rem(lon, 2)


def by_cell(pattern_row, cells):
    cell = lax.broadcasted_iota(jnp.int32, (cells, cells), 0)
    return jnp.where(pattern_row == cell, 1.0, 0.0).astype(bf16)


def position_by_row(cells, slots, blocks, row_dim):
    row = lax.broadcasted_iota(jnp.int32, (cells, cells), row_dim)
    position = lax.broadcasted_iota(jnp.int32, (cells, cells), 1 - row_dim)
    place = lax.rem(row, slots) * blocks + lax.div(row, slots)
    return jnp.where(place == position, 1.0, 0.0).astype(bf16)


def rim_cells(field_ref, row_ref, cols_ref):
    rows, cols, _ = field_ref.shape
    low, even = place()[0] == 0, place()[2] == 0
    row_ref[...] = jnp.where(low, field_ref[rows - 1], field_ref[0])
    first = jnp.concatenate([field_ref[row, 0:1] for row in range(rows)], axis=0)
    last = jnp.concatenate([field_ref[row, cols - 1 : cols] for row in range(rows)], axis=0)
    cols_ref[0] = jnp.where(even, last, first)
    cols_ref[1] = jnp.where(even, first, last)


def start_kernel(pattern_ref, rows_ref, field_ref, out_ref, row_ref, cols_ref):
    cells = rows_ref.shape[0]
    rim_cells(field_ref, row_ref, cols_ref)
    out_ref[...] = dot(by_cell(pattern_ref[...], cells), rows_ref[...], TN).astype(bf16)


def fill_pad(pad, field_ref, before_ref, after_ref, even_ref, odd_ref):
    rows, cols, _ = field_ref.shape
    before, after = before_ref[...].astype(f32), after_ref[...].astype(f32)
    pad[0, EDGE : EDGE + cols] = jnp.where(place()[0] != 0, before, jnp.zeros_like(before))
    pad[rows + 1, EDGE : EDGE + cols] = jnp.where(place()[1] != 0, after, jnp.zeros_like(after))
    for row in range(rows):
        pad[row + 1, EDGE : EDGE + cols] = field_ref[row].astype(f32)
    even, odd = even_ref[...].astype(f32), odd_ref[...].astype(f32)
    left = jnp.where(place()[2] == 0, odd, even)
    right = jnp.where(place()[2] == 0, even, odd)
    for row in range(rows + 2):
        pad[row, EDGE - 1 : EDGE] = left[row : row + 1]
        pad[row, EDGE + cols : EDGE + cols + 1] = right[row : row + 1]


def taps_row(pad, taps, row, cols, flip):
    summed = pad[row + 1, EDGE : EDGE + cols]
    for a in range(3):
        for b in range(3):
            tap = taps[2 - a, 2 - b : 3 - b] if flip else taps[a, b : b + 1]
            summed = summed + tap * pad[row + a, EDGE - 1 + b : EDGE - 1 + b + cols]
    return summed


def normalized(h):
    mean = jnp.mean(h, axis=-1, keepdims=True)
    centred = h - mean
    var = jnp.mean(centred * centred, axis=-1, keepdims=True)
    deviation = lax.rsqrt(var + epsilon)
    return centred * deviation, deviation


def enter_kernel(
    pattern_ref, field_ref, before_ref, after_ref, even_ref, odd_ref, taps_ref, gain_ref,
    h_ref, out_ref, pad, normed,
):
    rows, cols, _ = field_ref.shape
    fill_pad(pad, field_ref, before_ref, after_ref, even_ref, odd_ref)
    taps, gain = taps_ref[...], gain_ref[...]
    for row in range(rows):
        h = taps_row(pad, taps, row, cols, False).astype(bf16)
        h_ref[row * cols : (row + 1) * cols] = h
        xhat, _ = normalized(h.astype(f32))
        normed[row * cols : (row + 1) * cols] = (xhat * gain).astype(bf16)
    out_ref[...] = dot(by_cell(pattern_ref[...], rows * cols), normed[...], TN).astype(bf16)


def cot_kernel(slots, blocks, arrived_ref, out_weight_ref, grad_att_ref, cot_ref):
    cells = arrived_ref.shape[0]
    grouped = dot(position_by_row(cells, slots, blocks, 1), arrived_ref[...]).astype(bf16)
    grad_att_ref[...] = dot(out_weight_ref[...], grouped, NT).astype(bf16)
    cot_ref[...] = grouped.T


def low_lanes(dims):
    return lax.broadcasted_iota(jnp.int32, dims, len(dims) - 1) < GROUP


def pair_scores(left, right):
    both = dot(left, right, TN)
    return jnp.where(low_lanes((GROUP, PAIR)), both[:GROUP], both[GROUP:])


def pair_diagonal(compact):
    low = low_lanes((GROUP, PAIR))
    zero = jnp.zeros_like(compact)
    return jnp.concatenate([jnp.where(low, compact, zero), jnp.where(low, zero, compact)], axis=0)


def attention_kernel(
    slots, blocks, unroll,
    arrived_hbm, qkv_weight_hbm, bias_hbm, grad_att_hbm,
    grad_hbm, att_hbm,
    rows_buffer, qkv_weight, bias, grad_att, att_ref, qkv, grad_qkv, sems,
):
    cells, width = rows_buffer.shape
    copies = fetch(
        sems,
        (arrived_hbm, rows_buffer), (qkv_weight_hbm, qkv_weight), (bias_hbm, bias), (grad_att_hbm, grad_att),
    )
    gather = position_by_row(cells, slots, blocks, 1)
    copies[0].wait()
    grouped = dot(gather, rows_buffer[...]).astype(bf16)
    copies[1].wait()
    step = width // 2
    for at in range(0, 3 * width, step):
        qkv[at : at + step] = dot(qkv_weight[:, at : at + step], grouped, TT).astype(bf16)
    copies[2].wait()
    copies[3].wait()
    scale = HEAD_DIM ** (-0.5)

    def heads(step, carry):
        some = [
            (step * unroll + u, slice(pair * PAIR, (pair + 1) * PAIR))
            for u in range(unroll)
            for pair in range(cells // PAIR)
        ]

        def rows(part, e):
            return pl.ds(pl.multiple_of(part * width + e * HEAD_DIM, HEAD_DIM), HEAD_DIM)

        def q(e, at):
            return qkv[rows(0, e), at]

        def k(e, at):
            return qkv[rows(1, e), at]

        def v(e, at):
            return qkv[rows(2, e), at]

        def grad(e, at):
            return grad_att[rows(0, e), at]

        scores = [pair_scores(k(*x), q(*x)) * scale + bias[x[0]] for x in some]
        grad_probs = [pair_scores(v(*x), grad(*x)) for x in some]
        lifted = [jnp.exp(y - jnp.max(y, axis=0, keepdims=True)) for y in scores]
        probs = [y / jnp.sum(y, axis=0, keepdims=True) for y in lifted]
        probs_low = [pair_diagonal(y).astype(bf16) for y in probs]
        att = [dot(v(*x), y) for x, y in zip(some, probs_low)]
        to_value = [dot(grad(*x), y, NT) for x, y in zip(some, probs_low)]
        grad_scores = []
        for y, z in zip(probs, grad_probs):
            product = y * z
            inner = product - y * jnp.sum(product, axis=0, keepdims=True)
            grad_scores.append(pair_diagonal(inner).astype(bf16))
        to_query = [dot(k(*x), y) * scale for x, y in zip(some, grad_scores)]
        to_key = [dot(q(*x), y, NT) * scale for x, y in zip(some, grad_scores)]
        for i, (e, at) in enumerate(some):
            att_ref[rows(0, e), at] = att[i].astype(bf16)
            grad_qkv[rows(0, e), at] = to_query[i].astype(bf16)
            grad_qkv[rows(1, e), at] = to_key[i].astype(bf16)
            grad_qkv[rows(2, e), at] = to_value[i].astype(bf16)
        return carry

    if unroll == HEADS:
        heads(0, 0)
    else:
        lax.fori_loop(0, HEADS // unroll, heads, 0)
    last = pltpu.make_async_copy(att_ref, att_hbm, sems.at[1])
    last.start()
    grad = dot(qkv_weight[...], grad_qkv[...]).astype(bf16)
    rows_buffer[...] = dot(position_by_row(cells, slots, blocks, 0), grad, NT).astype(bf16)
    for copy in [last, *fetch(sems, (rows_buffer, grad_hbm))]:
        copy.wait()


def mix(slots, blocks, out_weight_ref, att_ref, mixed_ref):
    mixed = dot(out_weight_ref[...], att_ref[...], TN).astype(bf16)
    scatter = position_by_row(att_ref.shape[1], slots, blocks, 0)
    mixed_ref[...] = dot(scatter, mixed, NT).astype(bf16)


def products_kernel(slots, blocks, cot_ref, att_ref, out_weight_ref, mixed_ref, out_ref):
    out_ref[...] = dot(cot_ref[...], att_ref[...], NT).astype(bf16)
    mix(slots, blocks, out_weight_ref, att_ref, mixed_ref)


def halves_kernel(
    slots, blocks, cot_ref, att_ref, out_weight_ref, mixed_ref, kept_ref, sent_ref, part
):
    lats, chips, cols, rows = kept_ref.shape
    core = place()[2]
    for a in range(lats):
        part[...] = dot(cot_ref[...], att_ref[a * rows : (a + 1) * rows], NT).astype(bf16)
        for chip in range(chips):
            kept_ref[a, chip] = part[pl.ds(pl.multiple_of((2 * chip + core) * cols, 16), cols)]
            sent_ref[a, chip] = part[pl.ds(pl.multiple_of((2 * chip + 1 - core) * cols, 16), cols)]
    mix(slots, blocks, out_weight_ref, att_ref, mixed_ref)


def join_halves_kernel(kept_ref, met_ref, out_ref, sent_ref):
    lat = jnp.minimum(place()[0], 1)
    out_ref[...] = (kept_ref[lat].astype(f32) + met_ref[lat].astype(f32)).astype(bf16)
    sent_ref[...] = (kept_ref[1 - lat].astype(f32) + met_ref[1 - lat].astype(f32)).astype(bf16)


def leave_kernel(pattern_ref, mixed_ref, h_ref, out_ref):
    mixed = dot(by_cell(pattern_ref[...], h_ref.shape[0]), mixed_ref[...])
    out_ref[...] = (h_ref[...].astype(f32) + mixed).astype(bf16)


def return_kernel(
    pattern_ref, arrived_ref, h_ref, cot_ref, gain_ref,
    field_ref, before_ref, after_ref, even_ref, odd_ref,
    grad_ref, sums_ref, message_ref, columns_ref, pad, normed_grad,
):
    rows, cols, width = field_ref.shape
    fill_pad(pad, field_ref, before_ref, after_ref, even_ref, odd_ref)
    normed_grad[...] = dot(by_cell(pattern_ref[...], rows * cols), arrived_ref[...])
    gain = gain_ref[...]

    def fold(x):
        return jnp.sum(x.reshape(cols // 8, 8, width), axis=0)

    sums = [jnp.zeros((8, width), f32) for _ in range(10)]
    for row in range(rows):
        at = slice(row * cols, (row + 1) * cols)
        xhat, deviation = normalized(h_ref[at].astype(f32))
        grad = normed_grad[at]
        sums[9] = sums[9] + fold(grad * xhat)
        u = grad * gain
        inner = u - jnp.mean(u, axis=-1, keepdims=True)
        inner = inner - xhat * jnp.mean(u * xhat, axis=-1, keepdims=True)
        grad_h = (cot_ref[at].astype(f32) + deviation * inner).astype(bf16)
        grad_ref[row] = grad_h
        grad_h = grad_h.astype(f32)
        for a in range(3):
            for b in range(3):
                moved = pad[row + a, EDGE - 1 + b : EDGE - 1 + b + cols]
                sums[3 * a + b] = sums[3 * a + b] + fold(moved * grad_h)
    for i in range(10):
        sums_ref[i : i + 1] = jnp.sum(sums[i], axis=0, keepdims=True)
    sums_ref[10:16] = jnp.zeros((6, width), f32)
    rim_cells(grad_ref, message_ref.at[:cols], columns_ref)
    total = sums_ref[...]
    high = total.astype(bf16)
    message_ref[cols : cols + 16] = high
    message_ref[cols + 16 :] = (total - high.astype(f32)).astype(bf16)


def finish_kernel(scale, sums_ref, kept_ref, met_ref, taps_ref, gain_ref, project_ref):
    sums = sums_ref[...] * scale
    for a in range(3):
        taps_ref[a] = sums[3 * a : 3 * a + 3]
    gain_ref[...] = sums[9]
    project_ref[...] = (kept_ref[...].astype(f32) + met_ref[...].astype(f32)).T * scale


def spread_kernel(
    field_ref, before_ref, after_ref, even_ref, odd_ref, taps_ref, out_ref, pad
):
    rows, cols, _ = field_ref.shape
    fill_pad(pad, field_ref, before_ref, after_ref, even_ref, odd_ref)
    taps = taps_ref[...]
    for row in range(rows):
        out_ref[row] = taps_row(pad, taps, row, cols, True).astype(bf16)


def swap_pairs(size, bit):
    return [(i, i ^ bit) for i in range(size)]


def lat_rims(field, met):
    if lax.axis_size("lat") == 2:
        return met, met
    up = [(i, i + 1) for i in range(lax.axis_size("lat") - 1)]
    before = lax.ppermute(field[-1], "lat", up)
    after = lax.ppermute(field[0], "lat", [(j, i) for i, j in up])
    return before, after


def lon_rims(flags, rows, columns, riders=None):
    lon_count = lax.axis_size("lon")
    before, after = rows
    even = flags[2] == 0

    def column(which, last):
        at = before.shape[0] - 1

        def corner(row, there):
            cell = jnp.where(last, row[at:], row[:1])
            return jnp.where(there, cell, jnp.zeros_like(cell))

        return jnp.concatenate(
            [corner(before, flags[0] != 0), columns[which], corner(after, flags[1] != 0)], axis=0
        )

    sent = column(0, even)
    if riders is not None:
        sent = jnp.concatenate([riders, sent], axis=0)
    met_even = lax.ppermute(sent, "lon", swap_pairs(lon_count, 1))
    odd_pairs = [(i, (i + 1 if i % 2 else i - 1) % lon_count) for i in range(lon_count)]
    met_odd = lax.ppermute(column(1, jnp.logical_not(even)), "lon", odd_pairs)
    if riders is None:
        return met_even, met_odd
    count = riders.shape[0]
    return met_even[count:], met_odd, met_even[:count]


def exchange(rows):
    blocks = lax.axis_size("lat") * lax.axis_size("lon")
    cells, width = rows.shape
    sent = rows.reshape(blocks, cells // blocks, width)
    return lax.all_to_all(sent, AXES, split_axis=0, concat_axis=0, tiled=True).reshape(cells, width)


def attended_products(slots, blocks, flags, cot_cols, att, out_weight):
    width, cells = att.shape
    lat_count, lon_count = lax.axis_size("lat"), lax.axis_size("lon")
    rows, cols = width // lat_count, width // lon_count
    mixed_shape = shape((cells, width), bf16)
    if lat_count != 2 or lon_count % 4 or lon_count & (lon_count - 1) or rows % 128 or cols % 16:
        mixed, parts = call(
            lambda *refs: products_kernel(slots, blocks, *refs),
            "attended_products", [mixed_shape, shape((width, width), bf16)],
            [cot_cols, att, out_weight],
        )
        parts = parts.reshape(lon_count, cols, lat_count, rows).transpose(2, 0, 1, 3)
        parts = parts.reshape(lat_count * lon_count, cols, rows)
        parts = lax.all_to_all(parts, AXES, split_axis=0, concat_axis=0, tiled=True)
        return mixed, jnp.sum(parts.astype(f32), axis=0)
    halves = shape((lat_count, lon_count // 2, cols, rows), bf16)
    quarters = shape((lon_count // 2, cols, rows), bf16)
    mixed, kept, sent = call(
        lambda *refs: halves_kernel(slots, blocks, *refs),
        "attended_products", [mixed_shape, halves, halves],
        [cot_cols, att, out_weight],
        [pltpu.VMEM((width, rows), bf16)],
    )
    met = lax.ppermute(sent, "lon", swap_pairs(lon_count, 1))
    kept, sent = call(
        join_halves_kernel, "project_join", [quarters, quarters], [kept, met]
    )
    met = lax.ppermute(sent, "lat", swap_pairs(2, 1))
    parts = (kept.astype(f32) + met.astype(f32)).astype(bf16)
    kept, sent = halved(parts, 2)
    return mixed, (kept, lax.ppermute(sent, "lon", swap_pairs(lon_count, 2)))


def halved(parts, bit):
    mine = lax.rem(lax.div(lax.axis_index("lon"), bit), 2)
    pairs = parts.reshape(parts.shape[0] // 2, 2, *parts.shape[1:])
    kept = lax.dynamic_index_in_dim(pairs, mine, 1, keepdims=False)
    return kept, lax.dynamic_index_in_dim(pairs, 1 - mine, 1, keepdims=False)


def two_terms(x):
    high = x.astype(bf16)
    return jnp.concatenate([high, (x - high.astype(f32)).astype(bf16)], axis=0)


def one_term(x):
    half = x.shape[0] // 2
    return x[:half].astype(f32) + x[half:].astype(f32)


def total_over(axis, x):
    size, bit = lax.axis_size(axis), 1
    if size & (size - 1):
        return lax.psum(x, axis)
    while bit < size:
        x = x + lax.ppermute(x, axis, swap_pairs(size, bit))
        bit *= 2
    return x


def body(
    fields, conv_kernel, layer_norm_gain, qkv_weight, out_weight, score_bias, pattern, cotangent
):
    rows, cols, width = fields.shape
    cells = rows * cols
    lat_count, lon_count = lax.axis_size("lat"), lax.axis_size("lon")
    blocks = lat_count * lon_count
    slots = cells // blocks
    scale_everywhere = 1.0 / math.sqrt(cells * blocks)
    pattern_row = pattern.reshape(1, cells)
    gain = layer_norm_gain.reshape(1, width)
    cot_rows = cotangent.reshape(cells, width)
    bias = jnp.swapaxes(score_bias, 1, 2)
    bias = jnp.concatenate([bias, bias], axis=2)
    pad = pltpu.VMEM((rows + 2, cols + 2 * EDGE, width), f32)
    rows_shape = shape((cells, width), bf16)
    cols_shape = shape((width, cells), bf16)
    tall_shape = shape((3 * width, cells), bf16)

    flags = (
        lax.axis_index("lat"), lat_count - 1 - lax.axis_index("lat"), lax.rem(lax.axis_index("lon"), 2)
    )
    row_shape, columns_shape = shape((cols, width), bf16), shape((2, rows, width), bf16)

    cot_packed, row, columns = call(
        start_kernel, "start", [rows_shape, row_shape, columns_shape],
        [pattern_row, cot_rows, fields], mib=BIG,
    )
    met = lax.ppermute(row, "lat", swap_pairs(2, 1)) if lat_count == 2 else None
    cot_arrived = exchange(cot_packed)
    grad_att, cot_cols = call(
        lambda *refs: cot_kernel(slots, blocks, *refs),
        "cotangent_products", [cols_shape, cols_shape], [cot_arrived, out_weight], mib=BIG,
    )

    beside = lat_rims(fields, met)
    beside = (*beside, *lon_rims(flags, beside, columns))
    h, packed = call(
        enter_kernel, "convolve_normalize_pack", [rows_shape, rows_shape],
        [pattern_row, fields, *beside, conv_kernel, gain],
        [pad, pltpu.VMEM((cells, width), bf16)], mib=BIG,
    )
    arrived = exchange(packed)
    grad_grouped, att = pl.pallas_call(
        lambda *refs: attention_kernel(slots, blocks, UNROLL, *refs),
        name="attention",
        out_shape=[rows_shape, cols_shape],
        in_specs=[ANY] * 4,
        out_specs=[ANY] * 2,
        scratch_shapes=[
            pltpu.VMEM((cells, width), bf16), pltpu.VMEM(qkv_weight.shape, bf16),
            pltpu.VMEM(bias.shape, f32), pltpu.VMEM((width, cells), bf16),
            pltpu.VMEM((width, cells), bf16), pltpu.VMEM((3 * width, cells), bf16),
            pltpu.VMEM((3 * width, cells), bf16), pltpu.SemaphoreType.DMA((4,)),
        ],
        compiler_params=pltpu.CompilerParams(vmem_limit_bytes=BIG * 1024 * 1024),
        cost_estimate=pl.CostEstimate(
            flops=12_000_000_000, bytes_accessed=8_000_000, transcendentals=0
        ),
    )(arrived, qkv_weight, bias, grad_att)
    grad_home = exchange(grad_grouped)
    mixed, project = attended_products(slots, blocks, flags, cot_cols, att, out_weight)
    grad_home, mixed = lax.optimization_barrier((grad_home, mixed))
    mixed_home = exchange(mixed)

    grad_h, sums, message, columns = call(
        return_kernel, "normalize_back",
        [
            shape(fields.shape, bf16), shape((16, width), f32),
            shape((cols + 32, width), bf16), columns_shape,
        ],
        [pattern_row, grad_home, h, cot_rows, gain, fields, *beside],
        [pad, pltpu.VMEM((cells, width), f32)],
    )
    if lat_count == 2:
        met = lax.ppermute(message, "lat", swap_pairs(2, 1))
        sums = sums + one_term(met[cols:])
        beside = lat_rims(grad_h, met[:cols])
    else:
        sums = total_over("lat", sums)
        beside = lat_rims(grad_h, None)
    staged = isinstance(project, tuple)
    if staged:
        even, odd, met = lon_rims(flags, beside, columns, two_terms(sums))
        beside = (*beside, even, odd)
        sums = sums + one_term(met)
        sums = sums + lax.ppermute(sums, "lon", swap_pairs(lon_count, 2))
        sums, odd = lax.optimization_barrier((sums, odd))
        beside = (*beside[:2], even, odd)
        kept, met = project
        bit = 4
        while bit < lon_count:
            if 2 * bit == lon_count:
                sums, mixed_home = lax.optimization_barrier((sums, mixed_home))
            project = (kept.astype(f32) + met.astype(f32)).astype(bf16)
            kept, sent = halved(project, bit)
            high_low = two_terms(sums).reshape(-1, sent.shape[-1])
            sent = sent.reshape(-1, sent.shape[-1])
            met = lax.ppermute(
                jnp.concatenate([high_low, sent], axis=0), "lon", swap_pairs(lon_count, bit)
            )
            sums = sums + one_term(met[: high_low.shape[0]].reshape(2 * sums.shape[0], width))
            met = met[high_low.shape[0] :].reshape(kept.shape)
            bit *= 2
        kept, met = kept[0], met[0]
    else:
        beside = (*beside, *lon_rims(flags, beside, columns))
        sums = total_over("lon", sums)
        kept, met = project, jnp.zeros_like(project)
    grad_fields = call(
        spread_kernel, "convolve_back", [shape(fields.shape, bf16)],
        [grad_h, *beside, conv_kernel], [pad],
    )[0]
    block_out = call(leave_kernel, "block_out", [rows_shape], [pattern_row, mixed_home, h])[0]
    grad_kernel, gain_gradient, grad_project = call(
        lambda *refs: finish_kernel(scale_everywhere, *refs), "finish",
        [shape((3, 3, width), f32), shape((width,), f32), shape(kept.shape[::-1], f32)],
        [sums, kept, met],
    )
    return (
        block_out.reshape(rows, cols, width),
        grad_fields,
        grad_project,
        grad_kernel,
        gain_gradient,
    )


def solution(mesh):
    placed = (
        P("lat", "lon", None),
        P(),
        P(),
        P(),
        P(),
        P(),
        P("lat", "lon", None),
        P("lat", "lon", None),
    )
    return jax.shard_map(
        body,
        mesh=mesh,
        in_specs=placed,
        out_specs=(P("lat", "lon", None), P("lat", "lon", None), P("lat", "lon"), P(), P()),
        check_vma=False,
    )
```

```python
import math

import jax
import jax.numpy as jnp
from jax import lax
from jax.experimental import pallas as pl
from jax.experimental.pallas import tpu as pltpu
from jax.sharding import PartitionSpec as P

HEADS = 24
HEAD_DIM = 32
GROUP = 64
PAIR = 2 * GROUP
EDGE = 8
UNROLL = 24

epsilon = 1e-05
f32, bf16 = jnp.float32, jnp.bfloat16
AXES = ("lat", "lon")
NN = (((1,), (0,)), ((), ()))
NT = (((1,), (1,)), ((), ()))
TN = (((0,), (0,)), ((), ()))
TT = (((0,), (1,)), ((), ()))
VMEM = pl.BlockSpec(memory_space=pltpu.VMEM)
SMEM = pl.BlockSpec(memory_space=pltpu.SMEM)
ANY = pl.BlockSpec(memory_space=pl.ANY)
BIG = 60


def dot(a, b, dims=NN):
    return lax.dot_general(a, b, dims, preferred_element_type=f32)


def whole(x):
    return pl.BlockSpec(x.shape, lambda step: (0,) * len(x.shape))


def call(kernel, name, out_shape, operands, scratch=(), flops=0, specs=(), mib=40):
    size = sum(math.prod(x.shape) * x.dtype.itemsize for x in (*operands, *out_shape))
    specs = dict(specs)
    return pl.pallas_call(
        kernel,
        name=name,
        grid=(1,),
        out_shape=list(out_shape),
        in_specs=[specs.get(i, whole(x)) for i, x in enumerate(operands)],
        out_specs=[whole(x) for x in out_shape],
        scratch_shapes=list(scratch),
        compiler_params=pltpu.CompilerParams(vmem_limit_bytes=mib * 1024 * 1024),
        cost_estimate=pl.CostEstimate(flops=flops, bytes_accessed=size, transcendentals=0),
    )(*operands)


def fetch(sems, *pairs):
    copies = [pltpu.make_async_copy(x, y, sems.at[i]) for i, (x, y) in enumerate(pairs)]
    for copy in copies:
        copy.start()
    return copies


def shape(dims, dtype):
    return jax.ShapeDtypeStruct(dims, dtype)


def place():
    lat, lon = lax.axis_index("lat"), lax.axis_index("lon")
    return lat, lax.axis_size("lat") - 1 - lat, lax.rem(lon, 2)


def by_cell(pattern_row, cells):
    cell = lax.broadcasted_iota(jnp.int32, (cells, cells), 0)
    return jnp.where(pattern_row == cell, 1.0, 0.0).astype(bf16)


def position_by_row(cells, slots, blocks, row_dim):
    row = lax.broadcasted_iota(jnp.int32, (cells, cells), row_dim)
    position = lax.broadcasted_iota(jnp.int32, (cells, cells), 1 - row_dim)
    place = lax.rem(row, slots) * blocks + lax.div(row, slots)
    return jnp.where(place == position, 1.0, 0.0).astype(bf16)


def rim_cells(field_ref, row_ref, cols_ref):
    rows, cols, _ = field_ref.shape
    low, even = place()[0] == 0, place()[2] == 0
    row_ref[...] = jnp.where(low, field_ref[rows - 1], field_ref[0])
    first = jnp.concatenate([field_ref[row, 0:1] for row in range(rows)], axis=0)
    last = jnp.concatenate([field_ref[row, cols - 1 : cols] for row in range(rows)], axis=0)
    cols_ref[0] = jnp.where(even, last, first)
    cols_ref[1] = jnp.where(even, first, last)


def start_kernel(pattern_ref, rows_ref, field_ref, out_ref, row_ref, cols_ref):
    cells = rows_ref.shape[0]
    rim_cells(field_ref, row_ref, cols_ref)
    out_ref[...] = dot(by_cell(pattern_ref[...], cells), rows_ref[...], TN).astype(bf16)


def fill_pad(pad, field_ref, before_ref, after_ref, even_ref, odd_ref):
    rows, cols, _ = field_ref.shape
    before, after = before_ref[...].astype(f32), after_ref[...].astype(f32)
    pad[0, EDGE : EDGE + cols] = jnp.where(place()[0] != 0, before, jnp.zeros_like(before))
    pad[rows + 1, EDGE : EDGE + cols] = jnp.where(place()[1] != 0, after, jnp.zeros_like(after))
    for row in range(rows):
        pad[row + 1, EDGE : EDGE + cols] = field_ref[row].astype(f32)
    even, odd = even_ref[...].astype(f32), odd_ref[...].astype(f32)
    left = jnp.where(place()[2] == 0, odd, even)
    right = jnp.where(place()[2] == 0, even, odd)
    for row in range(rows + 2):
        pad[row, EDGE - 1 : EDGE] = left[row : row + 1]
        pad[row, EDGE + cols : EDGE + cols + 1] = right[row : row + 1]


def taps_row(pad, taps, row, cols, flip):
    summed = pad[row + 1, EDGE : EDGE + cols]
    for a in range(3):
        for b in range(3):
            tap = taps[2 - a, 2 - b : 3 - b] if flip else taps[a, b : b + 1]
            summed = summed + tap * pad[row + a, EDGE - 1 + b : EDGE - 1 + b + cols]
    return summed


def normalized(h):
    mean = jnp.mean(h, axis=-1, keepdims=True)
    centred = h - mean
    var = jnp.mean(centred * centred, axis=-1, keepdims=True)
    deviation = lax.rsqrt(var + epsilon)
    return centred * deviation, deviation


def enter_kernel(
    pattern_ref, field_ref, before_ref, after_ref, even_ref, odd_ref, taps_ref, gain_ref,
    h_ref, out_ref, pad, normed,
):
    rows, cols, _ = field_ref.shape
    fill_pad(pad, field_ref, before_ref, after_ref, even_ref, odd_ref)
    taps, gain = taps_ref[...], gain_ref[...]
    for row in range(rows):
        h = taps_row(pad, taps, row, cols, False).astype(bf16)
        h_ref[row * cols : (row + 1) * cols] = h
        xhat, _ = normalized(h.astype(f32))
        normed[row * cols : (row + 1) * cols] = (xhat * gain).astype(bf16)
    out_ref[...] = dot(by_cell(pattern_ref[...], rows * cols), normed[...], TN).astype(bf16)


def cot_kernel(slots, blocks, arrived_ref, out_weight_ref, grad_att_ref, cot_ref):
    cells = arrived_ref.shape[0]
    grouped = dot(position_by_row(cells, slots, blocks, 1), arrived_ref[...]).astype(bf16)
    grad_att_ref[...] = dot(out_weight_ref[...], grouped, NT).astype(bf16)
    cot_ref[...] = grouped.T


def low_lanes(dims):
    return lax.broadcasted_iota(jnp.int32, dims, len(dims) - 1) < GROUP


def pair_scores(left, right):
    both = dot(left, right, TN)
    return jnp.where(low_lanes((GROUP, PAIR)), both[:GROUP], both[GROUP:])


def pair_diagonal(compact):
    low = low_lanes((GROUP, PAIR))
    zero = jnp.zeros_like(compact)
    return jnp.concatenate([jnp.where(low, compact, zero), jnp.where(low, zero, compact)], axis=0)


def attention_kernel(
    slots, blocks, unroll,
    arrived_hbm, qkv_weight_hbm, bias_hbm, grad_att_hbm,
    grad_hbm, att_hbm,
    rows_buffer, qkv_weight, bias, grad_att, att_ref, qkv, grad_qkv, sems,
):
    cells, width = rows_buffer.shape
    copies = fetch(
        sems,
        (arrived_hbm, rows_buffer), (qkv_weight_hbm, qkv_weight), (bias_hbm, bias), (grad_att_hbm, grad_att),
    )
    gather = position_by_row(cells, slots, blocks, 1)
    copies[0].wait()
    grouped = dot(gather, rows_buffer[...]).astype(bf16)
    copies[1].wait()
    step = width // 2
    for at in range(0, 3 * width, step):
        qkv[at : at + step] = dot(qkv_weight[:, at : at + step], grouped, TT).astype(bf16)
    copies[2].wait()
    copies[3].wait()
    scale = HEAD_DIM ** (-0.5)

    def heads(step, carry):
        some = [
            (step * unroll + u, slice(pair * PAIR, (pair + 1) * PAIR))
            for u in range(unroll)
            for pair in range(cells // PAIR)
        ]

        def rows(part, e):
            return pl.ds(pl.multiple_of(part * width + e * HEAD_DIM, HEAD_DIM), HEAD_DIM)

        def q(e, at):
            return qkv[rows(0, e), at]

        def k(e, at):
            return qkv[rows(1, e), at]

        def v(e, at):
            return qkv[rows(2, e), at]

        def grad(e, at):
            return grad_att[rows(0, e), at]

        scores = [pair_scores(k(*x), q(*x)) * scale + bias[x[0]] for x in some]
        grad_probs = [pair_scores(v(*x), grad(*x)) for x in some]
        lifted = [jnp.exp(y - jnp.max(y, axis=0, keepdims=True)) for y in scores]
        probs = [y / jnp.sum(y, axis=0, keepdims=True) for y in lifted]
        probs_low = [pair_diagonal(y).astype(bf16) for y in probs]
        att = [dot(v(*x), y) for x, y in zip(some, probs_low)]
        to_value = [dot(grad(*x), y, NT) for x, y in zip(some, probs_low)]
        grad_scores = []
        for y, z in zip(probs, grad_probs):
            product = y * z
            inner = product - y * jnp.sum(product, axis=0, keepdims=True)
            grad_scores.append(pair_diagonal(inner).astype(bf16))
        to_query = [dot(k(*x), y) * scale for x, y in zip(some, grad_scores)]
        to_key = [dot(q(*x), y, NT) * scale for x, y in zip(some, grad_scores)]
        for i, (e, at) in enumerate(some):
            att_ref[rows(0, e), at] = att[i].astype(bf16)
            grad_qkv[rows(0, e), at] = to_query[i].astype(bf16)
            grad_qkv[rows(1, e), at] = to_key[i].astype(bf16)
            grad_qkv[rows(2, e), at] = to_value[i].astype(bf16)
        return carry

    if unroll == HEADS:
        heads(0, 0)
    else:
        lax.fori_loop(0, HEADS // unroll, heads, 0)
    last = pltpu.make_async_copy(att_ref, att_hbm, sems.at[1])
    last.start()
    grad = dot(qkv_weight[...], grad_qkv[...]).astype(bf16)
    rows_buffer[...] = dot(position_by_row(cells, slots, blocks, 0), grad, NT).astype(bf16)
    for copy in [last, *fetch(sems, (rows_buffer, grad_hbm))]:
        copy.wait()


def mix(slots, blocks, out_weight_ref, att_ref, mixed_ref):
    mixed = dot(out_weight_ref[...], att_ref[...], TN).astype(bf16)
    scatter = position_by_row(att_ref.shape[1], slots, blocks, 0)
    mixed_ref[...] = dot(scatter, mixed, NT).astype(bf16)


def products_kernel(slots, blocks, cot_ref, att_ref, out_weight_ref, mixed_ref, out_ref):
    out_ref[...] = dot(cot_ref[...], att_ref[...], NT).astype(bf16)
    mix(slots, blocks, out_weight_ref, att_ref, mixed_ref)


def halves_kernel(
    slots, blocks, cot_ref, att_ref, out_weight_ref, mixed_ref, kept_ref, sent_ref, part
):
    lats, chips, cols, rows = kept_ref.shape
    core = place()[2]
    for a in range(lats):
        part[...] = dot(cot_ref[...], att_ref[a * rows : (a + 1) * rows], NT).astype(bf16)
        for chip in range(chips):
            kept_ref[a, chip] = part[pl.ds(pl.multiple_of((2 * chip + core) * cols, 16), cols)]
            sent_ref[a, chip] = part[pl.ds(pl.multiple_of((2 * chip + 1 - core) * cols, 16), cols)]
    mix(slots, blocks, out_weight_ref, att_ref, mixed_ref)


def join_halves_kernel(kept_ref, met_ref, out_ref, sent_ref):
    lat = jnp.minimum(place()[0], 1)
    out_ref[...] = (kept_ref[lat].astype(f32) + met_ref[lat].astype(f32)).astype(bf16)
    sent_ref[...] = (kept_ref[1 - lat].astype(f32) + met_ref[1 - lat].astype(f32)).astype(bf16)


def leave_kernel(pattern_ref, mixed_ref, h_ref, out_ref):
    mixed = dot(by_cell(pattern_ref[...], h_ref.shape[0]), mixed_ref[...])
    out_ref[...] = (h_ref[...].astype(f32) + mixed).astype(bf16)


def return_kernel(
    pattern_ref, arrived_ref, h_ref, cot_ref, gain_ref,
    field_ref, before_ref, after_ref, even_ref, odd_ref,
    grad_ref, sums_ref, message_ref, columns_ref, pad, normed_grad,
):
    rows, cols, width = field_ref.shape
    fill_pad(pad, field_ref, before_ref, after_ref, even_ref, odd_ref)
    normed_grad[...] = dot(by_cell(pattern_ref[...], rows * cols), arrived_ref[...])
    gain = gain_ref[...]

    def fold(x):
        return jnp.sum(x.reshape(cols // 8, 8, width), axis=0)

    sums = [jnp.zeros((8, width), f32) for _ in range(10)]
    for row in range(rows):
        at = slice(row * cols, (row + 1) * cols)
        xhat, deviation = normalized(h_ref[at].astype(f32))
        grad = normed_grad[at]
        sums[9] = sums[9] + fold(grad * xhat)
        u = grad * gain
        inner = u - jnp.mean(u, axis=-1, keepdims=True)
        inner = inner - xhat * jnp.mean(u * xhat, axis=-1, keepdims=True)
        grad_h = (cot_ref[at].astype(f32) + deviation * inner).astype(bf16)
        grad_ref[row] = grad_h
        grad_h = grad_h.astype(f32)
        for a in range(3):
            for b in range(3):
                moved = pad[row + a, EDGE - 1 + b : EDGE - 1 + b + cols]
                sums[3 * a + b] = sums[3 * a + b] + fold(moved * grad_h)
    for i in range(10):
        sums_ref[i : i + 1] = jnp.sum(sums[i], axis=0, keepdims=True)
    sums_ref[10:16] = jnp.zeros((6, width), f32)
    rim_cells(grad_ref, message_ref.at[:cols], columns_ref)
    total = sums_ref[...]
    high = total.astype(bf16)
    message_ref[cols : cols + 16] = high
    message_ref[cols + 16 :] = (total - high.astype(f32)).astype(bf16)


def finish_kernel(scale, sums_ref, kept_ref, met_ref, taps_ref, gain_ref, project_ref):
    sums = sums_ref[...] * scale
    for a in range(3):
        taps_ref[a] = sums[3 * a : 3 * a + 3]
    gain_ref[...] = sums[9]
    project_ref[...] = (kept_ref[...].astype(f32) + met_ref[...].astype(f32)) * scale


def spread_kernel(
    field_ref, before_ref, after_ref, even_ref, odd_ref, taps_ref, out_ref, pad
):
    rows, cols, _ = field_ref.shape
    fill_pad(pad, field_ref, before_ref, after_ref, even_ref, odd_ref)
    taps = taps_ref[...]
    for row in range(rows):
        out_ref[row] = taps_row(pad, taps, row, cols, True).astype(bf16)


def swap_pairs(size, bit):
    return [(i, i ^ bit) for i in range(size)]


def lat_rims(field, met):
    if lax.axis_size("lat") == 2:
        return met, met
    up = [(i, i + 1) for i in range(lax.axis_size("lat") - 1)]
    before = lax.ppermute(field[-1], "lat", up)
    after = lax.ppermute(field[0], "lat", [(j, i) for i, j in up])
    return before, after


def lon_rims(flags, rows, columns, riders=None):
    lon_count = lax.axis_size("lon")
    before, after = rows
    even = flags[2] == 0

    def column(which, last):
        at = before.shape[0] - 1

        def corner(row, there):
            cell = jnp.where(last, row[at:], row[:1])
            return jnp.where(there, cell, jnp.zeros_like(cell))

        return jnp.concatenate(
            [corner(before, flags[0] != 0), columns[which], corner(after, flags[1] != 0)], axis=0
        )

    sent = column(0, even)
    if riders is not None:
        sent = jnp.concatenate([riders, sent], axis=0)
    met_even = lax.ppermute(sent, "lon", swap_pairs(lon_count, 1))
    odd_pairs = [(i, (i + 1 if i % 2 else i - 1) % lon_count) for i in range(lon_count)]
    met_odd = lax.ppermute(column(1, jnp.logical_not(even)), "lon", odd_pairs)
    if riders is None:
        return met_even, met_odd
    count = riders.shape[0]
    return met_even[count:], met_odd, met_even[:count]


def exchange(rows):
    blocks = lax.axis_size("lat") * lax.axis_size("lon")
    cells, width = rows.shape
    sent = rows.reshape(blocks, cells // blocks, width)
    return lax.all_to_all(sent, AXES, split_axis=0, concat_axis=0, tiled=True).reshape(cells, width)


def attended_products(slots, blocks, flags, cot_cols, att, out_weight):
    width, cells = att.shape
    lat_count, lon_count = lax.axis_size("lat"), lax.axis_size("lon")
    rows, cols = width // lat_count, width // lon_count
    mixed_shape = shape((cells, width), bf16)
    if lat_count != 2 or lon_count % 4 or lon_count & (lon_count - 1) or rows % 128 or cols % 16:
        mixed, parts = call(
            lambda *refs: products_kernel(slots, blocks, *refs),
            "attended_products", [mixed_shape, shape((width, width), bf16)],
            [cot_cols, att, out_weight],
        )
        parts = parts.reshape(lon_count, cols, lat_count, rows).transpose(2, 0, 1, 3)
        parts = parts.reshape(lat_count * lon_count, cols, rows)
        parts = lax.all_to_all(parts, AXES, split_axis=0, concat_axis=0, tiled=True)
        return mixed, jnp.sum(parts.astype(f32), axis=0)
    halves = shape((lat_count, lon_count // 2, cols, rows), bf16)
    quarters = shape((lon_count // 2, cols, rows), bf16)
    mixed, kept, sent = call(
        lambda *refs: halves_kernel(slots, blocks, *refs),
        "attended_products", [mixed_shape, halves, halves],
        [cot_cols, att, out_weight],
        [pltpu.VMEM((width, rows), bf16)],
    )
    met = lax.ppermute(sent, "lon", swap_pairs(lon_count, 1))
    kept, sent = call(
        join_halves_kernel, "project_join", [quarters, quarters], [kept, met]
    )
    met = lax.ppermute(sent, "lat", swap_pairs(2, 1))
    parts = (kept.astype(f32) + met.astype(f32)).astype(bf16)
    kept, sent = halved(parts, 2)
    return mixed, (kept, lax.ppermute(sent, "lon", swap_pairs(lon_count, 2)))


def halved(parts, bit):
    mine = lax.rem(lax.div(lax.axis_index("lon"), bit), 2)
    pairs = parts.reshape(parts.shape[0] // 2, 2, *parts.shape[1:])
    kept = lax.dynamic_index_in_dim(pairs, mine, 1, keepdims=False)
    return kept, lax.dynamic_index_in_dim(pairs, 1 - mine, 1, keepdims=False)


def two_terms(x):
    high = x.astype(bf16)
    return jnp.concatenate([high, (x - high.astype(f32)).astype(bf16)], axis=0)


def one_term(x):
    half = x.shape[0] // 2
    return x[:half].astype(f32) + x[half:].astype(f32)


def total_over(axis, x):
    size, bit = lax.axis_size(axis), 1
    if size & (size - 1):
        return lax.psum(x, axis)
    while bit < size:
        x = x + lax.ppermute(x, axis, swap_pairs(size, bit))
        bit *= 2
    return x


def body(
    fields, conv_kernel, layer_norm_gain, qkv_weight, out_weight, score_bias, pattern, cotangent
):
    rows, cols, width = fields.shape
    cells = rows * cols
    lat_count, lon_count = lax.axis_size("lat"), lax.axis_size("lon")
    blocks = lat_count * lon_count
    slots = cells // blocks
    scale_everywhere = 1.0 / math.sqrt(cells * blocks)
    pattern_row = pattern.reshape(1, cells)
    gain = layer_norm_gain.reshape(1, width)
    cot_rows = cotangent.reshape(cells, width)
    bias = jnp.swapaxes(score_bias, 1, 2)
    bias = jnp.concatenate([bias, bias], axis=2)
    pad = pltpu.VMEM((rows + 2, cols + 2 * EDGE, width), f32)
    rows_shape = shape((cells, width), bf16)
    cols_shape = shape((width, cells), bf16)
    tall_shape = shape((3 * width, cells), bf16)

    flags = (
        lax.axis_index("lat"), lat_count - 1 - lax.axis_index("lat"), lax.rem(lax.axis_index("lon"), 2)
    )
    row_shape, columns_shape = shape((cols, width), bf16), shape((2, rows, width), bf16)

    cot_packed, row, columns = call(
        start_kernel, "start", [rows_shape, row_shape, columns_shape],
        [pattern_row, cot_rows, fields], mib=BIG,
    )
    met = lax.ppermute(row, "lat", swap_pairs(2, 1)) if lat_count == 2 else None
    cot_arrived = exchange(cot_packed)
    grad_att, cot_cols = call(
        lambda *refs: cot_kernel(slots, blocks, *refs),
        "cotangent_products", [cols_shape, cols_shape], [cot_arrived, out_weight], mib=BIG,
    )

    beside = lat_rims(fields, met)
    beside = (*beside, *lon_rims(flags, beside, columns))
    h, packed = call(
        enter_kernel, "convolve_normalize_pack", [rows_shape, rows_shape],
        [pattern_row, fields, *beside, conv_kernel, gain],
        [pad, pltpu.VMEM((cells, width), bf16)], mib=BIG,
    )
    arrived = exchange(packed)
    grad_grouped, att = pl.pallas_call(
        lambda *refs: attention_kernel(slots, blocks, UNROLL, *refs),
        name="attention",
        out_shape=[rows_shape, cols_shape],
        in_specs=[ANY] * 4,
        out_specs=[ANY] * 2,
        scratch_shapes=[
            pltpu.VMEM((cells, width), bf16), pltpu.VMEM(qkv_weight.shape, bf16),
            pltpu.VMEM(bias.shape, f32), pltpu.VMEM((width, cells), bf16),
            pltpu.VMEM((width, cells), bf16), pltpu.VMEM((3 * width, cells), bf16),
            pltpu.VMEM((3 * width, cells), bf16), pltpu.SemaphoreType.DMA((4,)),
        ],
        compiler_params=pltpu.CompilerParams(vmem_limit_bytes=BIG * 1024 * 1024),
        cost_estimate=pl.CostEstimate(
            flops=12_000_000_000, bytes_accessed=8_000_000, transcendentals=0
        ),
    )(arrived, qkv_weight, bias, grad_att)
    grad_home = exchange(grad_grouped)
    mixed, project = attended_products(slots, blocks, flags, cot_cols, att, out_weight)
    grad_home, mixed = lax.optimization_barrier((grad_home, mixed))
    mixed_home = exchange(mixed)

    grad_h, sums, message, columns = call(
        return_kernel, "normalize_back",
        [
            shape(fields.shape, bf16), shape((16, width), f32),
            shape((cols + 32, width), bf16), columns_shape,
        ],
        [pattern_row, grad_home, h, cot_rows, gain, fields, *beside],
        [pad, pltpu.VMEM((cells, width), f32)],
    )
    if lat_count == 2:
        met = lax.ppermute(message, "lat", swap_pairs(2, 1))
        sums = sums + one_term(met[cols:])
        beside = lat_rims(grad_h, met[:cols])
    else:
        sums = total_over("lat", sums)
        beside = lat_rims(grad_h, None)
    staged = isinstance(project, tuple)
    if staged:
        even, odd, met = lon_rims(flags, beside, columns, two_terms(sums))
        beside = (*beside, even, odd)
        sums = sums + one_term(met)
        sums = sums + lax.ppermute(sums, "lon", swap_pairs(lon_count, 2))
        sums, odd = lax.optimization_barrier((sums, odd))
        beside = (*beside[:2], even, odd)
        kept, met = project
        bit = 4
        while bit < lon_count:
            if 2 * bit == lon_count:
                sums, mixed_home = lax.optimization_barrier((sums, mixed_home))
            project = (kept.astype(f32) + met.astype(f32)).astype(bf16)
            kept, sent = halved(project, bit)
            high_low = two_terms(sums).reshape(-1, sent.shape[-1])
            sent = sent.reshape(-1, sent.shape[-1])
            met = lax.ppermute(
                jnp.concatenate([high_low, sent], axis=0), "lon", swap_pairs(lon_count, bit)
            )
            sums = sums + one_term(met[: high_low.shape[0]].reshape(2 * sums.shape[0], width))
            met = met[high_low.shape[0] :].reshape(kept.shape)
            bit *= 2
        kept, met = kept[0], met[0]
    else:
        beside = (*beside, *lon_rims(flags, beside, columns))
        sums = total_over("lon", sums)
        kept, met = project, jnp.zeros_like(project)
    grad_fields = call(
        spread_kernel, "convolve_back", [shape(fields.shape, bf16)],
        [grad_h, *beside, conv_kernel], [pad],
    )[0]
    block_out = call(leave_kernel, "block_out", [rows_shape], [pattern_row, mixed_home, h])[0]
    grad_kernel, gain_gradient, grad_project = call(
        lambda *refs: finish_kernel(scale_everywhere, *refs), "finish",
        [shape((3, 3, width), f32), shape((width,), f32), shape(kept.shape, f32)],
        [sums, kept, met],
    )
    return (
        block_out.reshape(rows, cols, width),
        grad_fields,
        grad_project.T,
        grad_kernel,
        gain_gradient,
    )


def solution(mesh):
    placed = (
        P("lat", "lon", None),
        P(),
        P(),
        P(),
        P(),
        P(),
        P("lat", "lon", None),
        P("lat", "lon", None),
    )
    return jax.shard_map(
        body,
        mesh=mesh,
        in_specs=placed,
        out_specs=(P("lat", "lon", None), P("lat", "lon", None), P("lat", "lon"), P(), P()),
        check_vma=False,
    )
```

```python
import math

import jax
import jax.numpy as jnp
from jax import lax
from jax.experimental import pallas as pl
from jax.experimental.pallas import tpu as pltpu
from jax.sharding import PartitionSpec as P

HEADS = 24
HEAD_DIM = 32
GROUP = 64
PAIR = 2 * GROUP
EDGE = 8
UNROLL = 24

epsilon = 1e-05
f32, bf16 = jnp.float32, jnp.bfloat16
AXES = ("lat", "lon")
NN = (((1,), (0,)), ((), ()))
NT = (((1,), (1,)), ((), ()))
TN = (((0,), (0,)), ((), ()))
TT = (((0,), (1,)), ((), ()))
VMEM = pl.BlockSpec(memory_space=pltpu.VMEM)
SMEM = pl.BlockSpec(memory_space=pltpu.SMEM)
ANY = pl.BlockSpec(memory_space=pl.ANY)
BIG = 60


def dot(a, b, dims=NN):
    return lax.dot_general(a, b, dims, preferred_element_type=f32)


def whole(x):
    return pl.BlockSpec(x.shape, lambda step: (0,) * len(x.shape))


def call(kernel, name, out_shape, operands, scratch=(), flops=0, specs=(), mib=40):
    size = sum(math.prod(x.shape) * x.dtype.itemsize for x in (*operands, *out_shape))
    specs = dict(specs)
    return pl.pallas_call(
        kernel,
        name=name,
        grid=(1,),
        out_shape=list(out_shape),
        in_specs=[specs.get(i, whole(x)) for i, x in enumerate(operands)],
        out_specs=[whole(x) for x in out_shape],
        scratch_shapes=list(scratch),
        compiler_params=pltpu.CompilerParams(vmem_limit_bytes=mib * 1024 * 1024),
        cost_estimate=pl.CostEstimate(flops=flops, bytes_accessed=size, transcendentals=0),
    )(*operands)


def fetch(sems, *pairs):
    copies = [pltpu.make_async_copy(x, y, sems.at[i]) for i, (x, y) in enumerate(pairs)]
    for copy in copies:
        copy.start()
    return copies


def shape(dims, dtype):
    return jax.ShapeDtypeStruct(dims, dtype)


def place():
    lat, lon = lax.axis_index("lat"), lax.axis_index("lon")
    return lat, lax.axis_size("lat") - 1 - lat, lax.rem(lon, 2)


def by_cell(pattern_row, cells):
    cell = lax.broadcasted_iota(jnp.int32, (cells, cells), 0)
    return jnp.where(pattern_row == cell, 1.0, 0.0).astype(bf16)


def position_by_row(cells, slots, blocks, row_dim):
    row = lax.broadcasted_iota(jnp.int32, (cells, cells), row_dim)
    position = lax.broadcasted_iota(jnp.int32, (cells, cells), 1 - row_dim)
    place = lax.rem(row, slots) * blocks + lax.div(row, slots)
    return jnp.where(place == position, 1.0, 0.0).astype(bf16)


def rim_cells(field_ref, row_ref, cols_ref):
    rows, cols, _ = field_ref.shape
    low, even = place()[0] == 0, place()[2] == 0
    row_ref[...] = jnp.where(low, field_ref[rows - 1], field_ref[0])
    first = jnp.concatenate([field_ref[row, 0:1] for row in range(rows)], axis=0)
    last = jnp.concatenate([field_ref[row, cols - 1 : cols] for row in range(rows)], axis=0)
    cols_ref[0] = jnp.where(even, last, first)
    cols_ref[1] = jnp.where(even, first, last)


def start_kernel(pattern_ref, rows_ref, field_ref, out_ref, row_ref, cols_ref):
    cells = rows_ref.shape[0]
    rim_cells(field_ref, row_ref, cols_ref)
    out_ref[...] = dot(by_cell(pattern_ref[...], cells), rows_ref[...], TN).astype(bf16)


def fill_pad(pad, field_ref, before_ref, after_ref, even_ref, odd_ref):
    rows, cols, _ = field_ref.shape
    before, after = before_ref[...].astype(f32), after_ref[...].astype(f32)
    pad[0, EDGE : EDGE + cols] = jnp.where(place()[0] != 0, before, jnp.zeros_like(before))
    pad[rows + 1, EDGE : EDGE + cols] = jnp.where(place()[1] != 0, after, jnp.zeros_like(after))
    for row in range(rows):
        pad[row + 1, EDGE : EDGE + cols] = field_ref[row].astype(f32)
    even, odd = even_ref[...].astype(f32), odd_ref[...].astype(f32)
    left = jnp.where(place()[2] == 0, odd, even)
    right = jnp.where(place()[2] == 0, even, odd)
    for row in range(rows + 2):
        pad[row, EDGE - 1 : EDGE] = left[row : row + 1]
        pad[row, EDGE + cols : EDGE + cols + 1] = right[row : row + 1]


def taps_row(pad, taps, row, cols, flip):
    summed = pad[row + 1, EDGE : EDGE + cols]
    for a in range(3):
        for b in range(3):
            tap = taps[2 - a, 2 - b : 3 - b] if flip else taps[a, b : b + 1]
            summed = summed + tap * pad[row + a, EDGE - 1 + b : EDGE - 1 + b + cols]
    return summed


def normalized(h):
    mean = jnp.mean(h, axis=-1, keepdims=True)
    centred = h - mean
    var = jnp.mean(centred * centred, axis=-1, keepdims=True)
    deviation = lax.rsqrt(var + epsilon)
    return centred * deviation, deviation


def enter_kernel(
    pattern_ref, field_ref, before_ref, after_ref, even_ref, odd_ref, taps_ref, gain_ref,
    h_ref, out_ref, pad, normed,
):
    rows, cols, _ = field_ref.shape
    fill_pad(pad, field_ref, before_ref, after_ref, even_ref, odd_ref)
    taps, gain = taps_ref[...], gain_ref[...]
    for row in range(rows):
        h = taps_row(pad, taps, row, cols, False).astype(bf16)
        h_ref[row * cols : (row + 1) * cols] = h
        xhat, _ = normalized(h.astype(f32))
        normed[row * cols : (row + 1) * cols] = (xhat * gain).astype(bf16)
    out_ref[...] = dot(by_cell(pattern_ref[...], rows * cols), normed[...], TN).astype(bf16)


def cot_kernel(slots, blocks, arrived_ref, out_weight_ref, grad_att_ref, cot_ref):
    cells = arrived_ref.shape[0]
    grouped = dot(position_by_row(cells, slots, blocks, 1), arrived_ref[...]).astype(bf16)
    grad_att_ref[...] = dot(out_weight_ref[...], grouped, NT).astype(bf16)
    cot_ref[...] = grouped.T


def low_lanes(dims):
    return lax.broadcasted_iota(jnp.int32, dims, len(dims) - 1) < GROUP


def pair_scores(left, right):
    both = dot(left, right, TN)
    return jnp.where(low_lanes((GROUP, PAIR)), both[:GROUP], both[GROUP:])


def pair_diagonal(compact):
    low = low_lanes((GROUP, PAIR))
    zero = jnp.zeros_like(compact)
    return jnp.concatenate([jnp.where(low, compact, zero), jnp.where(low, zero, compact)], axis=0)


def attention_kernel(
    slots, blocks, unroll,
    arrived_hbm, qkv_weight_hbm, bias_hbm, grad_att_hbm,
    grad_hbm, att_hbm, att_sent_hbm,
    rows_buffer, qkv_weight, bias, grad_att, att_ref, qkv, grad_qkv, sems,
):
    cells, width = rows_buffer.shape
    copies = fetch(
        sems,
        (arrived_hbm, rows_buffer), (qkv_weight_hbm, qkv_weight), (bias_hbm, bias), (grad_att_hbm, grad_att),
    )
    gather = position_by_row(cells, slots, blocks, 1)
    copies[0].wait()
    grouped = dot(gather, rows_buffer[...]).astype(bf16)
    copies[1].wait()
    step = width // 2
    for at in range(0, 3 * width, step):
        qkv[at : at + step] = dot(qkv_weight[:, at : at + step], grouped, TT).astype(bf16)
    copies[2].wait()
    copies[3].wait()
    scale = HEAD_DIM ** (-0.5)

    def heads(step, carry):
        some = [
            (step * unroll + u, slice(pair * PAIR, (pair + 1) * PAIR))
            for u in range(unroll)
            for pair in range(cells // PAIR)
        ]

        def rows(part, e):
            return pl.ds(pl.multiple_of(part * width + e * HEAD_DIM, HEAD_DIM), HEAD_DIM)

        def q(e, at):
            return qkv[rows(0, e), at]

        def k(e, at):
            return qkv[rows(1, e), at]

        def v(e, at):
            return qkv[rows(2, e), at]

        def grad(e, at):
            return grad_att[rows(0, e), at]

        scores = [pair_scores(k(*x), q(*x)) * scale + bias[x[0]] for x in some]
        grad_probs = [pair_scores(v(*x), grad(*x)) for x in some]
        lifted = [jnp.exp(y - jnp.max(y, axis=0, keepdims=True)) for y in scores]
        probs = [y / jnp.sum(y, axis=0, keepdims=True) for y in lifted]
        probs_low = [pair_diagonal(y).astype(bf16) for y in probs]
        att = [dot(v(*x), y) for x, y in zip(some, probs_low)]
        to_value = [dot(grad(*x), y, NT) for x, y in zip(some, probs_low)]
        grad_scores = []
        for y, z in zip(probs, grad_probs):
            product = y * z
            inner = product - y * jnp.sum(product, axis=0, keepdims=True)
            grad_scores.append(pair_diagonal(inner).astype(bf16))
        to_query = [dot(k(*x), y) * scale for x, y in zip(some, grad_scores)]
        to_key = [dot(q(*x), y, NT) * scale for x, y in zip(some, grad_scores)]
        for i, (e, at) in enumerate(some):
            att_ref[rows(0, e), at] = att[i].astype(bf16)
            grad_qkv[rows(0, e), at] = to_query[i].astype(bf16)
            grad_qkv[rows(1, e), at] = to_key[i].astype(bf16)
            grad_qkv[rows(2, e), at] = to_value[i].astype(bf16)
        return carry

    if unroll == HEADS:
        heads(0, 0)
    else:
        lax.fori_loop(0, HEADS // unroll, heads, 0)
    sent = att_sent_hbm.shape[0]
    other = pl.multiple_of((1 - jnp.minimum(place()[0], 1)) * sent, 16)
    leaving = fetch(sems, (att_ref.at[pl.ds(other, sent)], att_sent_hbm), (att_ref, att_hbm))
    grad = dot(qkv_weight[...], grad_qkv[...]).astype(bf16)
    rows_buffer[...] = dot(position_by_row(cells, slots, blocks, 0), grad, NT).astype(bf16)
    for copy in [*leaving, *fetch(sems.at[pl.ds(2, 1)], (rows_buffer, grad_hbm))]:
        copy.wait()


def mix(slots, blocks, out_weight_ref, att_ref, mixed_ref):
    mixed = dot(out_weight_ref[...], att_ref[...], TN).astype(bf16)
    scatter = position_by_row(att_ref.shape[1], slots, blocks, 0)
    mixed_ref[...] = dot(scatter, mixed, NT).astype(bf16)


def products_kernel(slots, blocks, cot_ref, att_ref, out_weight_ref, mixed_ref, out_ref):
    out_ref[...] = dot(cot_ref[...], att_ref[...], NT).astype(bf16)
    mix(slots, blocks, out_weight_ref, att_ref, mixed_ref)


def mix_kernel(slots, blocks, att_ref, out_weight_ref, mixed_ref):
    mix(slots, blocks, out_weight_ref, att_ref, mixed_ref)


def halves_kernel(cot_ref, cot_met_ref, att_ref, att_met_ref, kept_ref, sent_ref, part):
    chips, cols, rows = kept_ref.shape
    lat, _, core = place()
    mine = att_ref[pl.ds(pl.multiple_of(jnp.minimum(lat, 1) * rows, 16), rows)]
    total = dot(cot_ref[...], mine, NT) + dot(cot_met_ref[...], att_met_ref[...], NT)
    part[...] = total.astype(bf16)
    for chip in range(chips):
        kept_ref[chip] = part[pl.ds(pl.multiple_of((2 * chip + core) * cols, 16), cols)]
        sent_ref[chip] = part[pl.ds(pl.multiple_of((2 * chip + 1 - core) * cols, 16), cols)]


def leave_kernel(pattern_ref, mixed_ref, h_ref, out_ref):
    mixed = dot(by_cell(pattern_ref[...], h_ref.shape[0]), mixed_ref[...])
    out_ref[...] = (h_ref[...].astype(f32) + mixed).astype(bf16)


def return_kernel(
    pattern_ref, arrived_ref, h_ref, cot_ref, gain_ref,
    field_ref, before_ref, after_ref, even_ref, odd_ref,
    grad_ref, sums_ref, message_ref, columns_ref, pad, normed_grad,
):
    rows, cols, width = field_ref.shape
    fill_pad(pad, field_ref, before_ref, after_ref, even_ref, odd_ref)
    normed_grad[...] = dot(by_cell(pattern_ref[...], rows * cols), arrived_ref[...])
    gain = gain_ref[...]

    def fold(x):
        return jnp.sum(x.reshape(cols // 8, 8, width), axis=0)

    sums = [jnp.zeros((8, width), f32) for _ in range(10)]
    for row in range(rows):
        at = slice(row * cols, (row + 1) * cols)
        xhat, deviation = normalized(h_ref[at].astype(f32))
        grad = normed_grad[at]
        sums[9] = sums[9] + fold(grad * xhat)
        u = grad * gain
        inner = u - jnp.mean(u, axis=-1, keepdims=True)
        inner = inner - xhat * jnp.mean(u * xhat, axis=-1, keepdims=True)
        grad_h = (cot_ref[at].astype(f32) + deviation * inner).astype(bf16)
        grad_ref[row] = grad_h
        grad_h = grad_h.astype(f32)
        for a in range(3):
            for b in range(3):
                moved = pad[row + a, EDGE - 1 + b : EDGE - 1 + b + cols]
                sums[3 * a + b] = sums[3 * a + b] + fold(moved * grad_h)
    for i in range(10):
        sums_ref[i : i + 1] = jnp.sum(sums[i], axis=0, keepdims=True)
    sums_ref[10:16] = jnp.zeros((6, width), f32)
    rim_cells(grad_ref, message_ref.at[:cols], columns_ref)
    total = sums_ref[...]
    high = total.astype(bf16)
    message_ref[cols : cols + 16] = high
    message_ref[cols + 16 :] = (total - high.astype(f32)).astype(bf16)


def finish_kernel(scale, sums_ref, kept_ref, met_ref, taps_ref, gain_ref, project_ref):
    sums = sums_ref[...] * scale
    for a in range(3):
        taps_ref[a] = sums[3 * a : 3 * a + 3]
    gain_ref[...] = sums[9]
    project_ref[...] = (kept_ref[...].astype(f32) + met_ref[...].astype(f32)) * scale


def spread_kernel(
    field_ref, before_ref, after_ref, even_ref, odd_ref, taps_ref, out_ref, pad
):
    rows, cols, _ = field_ref.shape
    fill_pad(pad, field_ref, before_ref, after_ref, even_ref, odd_ref)
    taps = taps_ref[...]
    for row in range(rows):
        out_ref[row] = taps_row(pad, taps, row, cols, True).astype(bf16)


def swap_pairs(size, bit):
    return [(i, i ^ bit) for i in range(size)]


def lat_rims(field, met):
    if lax.axis_size("lat") == 2:
        return met, met
    up = [(i, i + 1) for i in range(lax.axis_size("lat") - 1)]
    before = lax.ppermute(field[-1], "lat", up)
    after = lax.ppermute(field[0], "lat", [(j, i) for i, j in up])
    return before, after


def lon_rims(flags, rows, columns, riders=None):
    lon_count = lax.axis_size("lon")
    before, after = rows
    even = flags[2] == 0

    def column(which, last):
        at = before.shape[0] - 1

        def corner(row, there):
            cell = jnp.where(last, row[at:], row[:1])
            return jnp.where(there, cell, jnp.zeros_like(cell))

        return jnp.concatenate(
            [corner(before, flags[0] != 0), columns[which], corner(after, flags[1] != 0)], axis=0
        )

    sent = column(0, even)
    if riders is not None:
        sent = jnp.concatenate([riders, sent], axis=0)
    met_even = lax.ppermute(sent, "lon", swap_pairs(lon_count, 1))
    odd_pairs = [(i, (i + 1 if i % 2 else i - 1) % lon_count) for i in range(lon_count)]
    met_odd = lax.ppermute(column(1, jnp.logical_not(even)), "lon", odd_pairs)
    if riders is None:
        return met_even, met_odd
    count = riders.shape[0]
    return met_even[count:], met_odd, met_even[:count]


def exchange(rows):
    blocks = lax.axis_size("lat") * lax.axis_size("lon")
    cells, width = rows.shape
    sent = rows.reshape(blocks, cells // blocks, width)
    return lax.all_to_all(sent, AXES, split_axis=0, concat_axis=0, tiled=True).reshape(cells, width)


def attended_products(slots, blocks, cot_cols, cot_met, att, att_sent, out_weight):
    width, cells = att.shape
    lat_count, lon_count = lax.axis_size("lat"), lax.axis_size("lon")
    rows, cols = width // lat_count, width // lon_count
    mixed_shape = shape((cells, width), bf16)
    if cot_met is None:
        mixed, parts = call(
            lambda *refs: products_kernel(slots, blocks, *refs),
            "attended_products", [mixed_shape, shape((width, width), bf16)],
            [cot_cols, att, out_weight],
        )
        parts = parts.reshape(lon_count, cols, lat_count, rows).transpose(2, 0, 1, 3)
        parts = parts.reshape(lat_count * lon_count, cols, rows)
        parts = lax.all_to_all(parts, AXES, split_axis=0, concat_axis=0, tiled=True)
        return mixed, jnp.sum(parts.astype(f32), axis=0)
    mixed = call(
        lambda *refs: mix_kernel(slots, blocks, *refs), "mix", [mixed_shape], [att, out_weight]
    )[0]
    att_met = lax.ppermute(att_sent, "lat", swap_pairs(2, 1))
    halves = shape((lon_count // 2, cols, rows), bf16)
    kept, sent = call(
        halves_kernel, "project_gradient", [halves, halves], [cot_cols, cot_met, att, att_met],
        [pltpu.VMEM((width, rows), bf16)],
    )
    met = lax.ppermute(sent, "lon", swap_pairs(lon_count, 1))
    parts = (kept.astype(f32) + met.astype(f32)).astype(bf16)
    kept, sent = halved(parts, 2)
    return mixed, (kept, lax.ppermute(sent, "lon", swap_pairs(lon_count, 2)))


def halved(parts, bit):
    mine = lax.rem(lax.div(lax.axis_index("lon"), bit), 2)
    pairs = parts.reshape(parts.shape[0] // 2, 2, *parts.shape[1:])
    kept = lax.dynamic_index_in_dim(pairs, mine, 1, keepdims=False)
    return kept, lax.dynamic_index_in_dim(pairs, 1 - mine, 1, keepdims=False)


def two_terms(x):
    high = x.astype(bf16)
    return jnp.concatenate([high, (x - high.astype(f32)).astype(bf16)], axis=0)


def one_term(x):
    half = x.shape[0] // 2
    return x[:half].astype(f32) + x[half:].astype(f32)


def total_over(axis, x):
    size, bit = lax.axis_size(axis), 1
    if size & (size - 1):
        return lax.psum(x, axis)
    while bit < size:
        x = x + lax.ppermute(x, axis, swap_pairs(size, bit))
        bit *= 2
    return x


def body(
    fields, conv_kernel, layer_norm_gain, qkv_weight, out_weight, score_bias, pattern, cotangent
):
    rows, cols, width = fields.shape
    cells = rows * cols
    lat_count, lon_count = lax.axis_size("lat"), lax.axis_size("lon")
    blocks = lat_count * lon_count
    slots = cells // blocks
    scale_everywhere = 1.0 / math.sqrt(cells * blocks)
    pattern_row = pattern.reshape(1, cells)
    gain = layer_norm_gain.reshape(1, width)
    cot_rows = cotangent.reshape(cells, width)
    bias = jnp.swapaxes(score_bias, 1, 2)
    bias = jnp.concatenate([bias, bias], axis=2)
    pad = pltpu.VMEM((rows + 2, cols + 2 * EDGE, width), f32)
    rows_shape = shape((cells, width), bf16)
    cols_shape = shape((width, cells), bf16)
    tall_shape = shape((3 * width, cells), bf16)

    flags = (
        lax.axis_index("lat"), lat_count - 1 - lax.axis_index("lat"), lax.rem(lax.axis_index("lon"), 2)
    )
    row_shape, columns_shape = shape((cols, width), bf16), shape((2, rows, width), bf16)

    cot_packed, row, columns = call(
        start_kernel, "start", [rows_shape, row_shape, columns_shape],
        [pattern_row, cot_rows, fields], mib=BIG,
    )
    met = lax.ppermute(row, "lat", swap_pairs(2, 1)) if lat_count == 2 else None
    cot_arrived = exchange(cot_packed)
    grad_att, cot_cols = call(
        lambda *refs: cot_kernel(slots, blocks, *refs),
        "cotangent_products", [cols_shape, cols_shape], [cot_arrived, out_weight], mib=BIG,
    )

    staged = lat_count == 2 and lon_count % 4 == 0 and lon_count & (lon_count - 1) == 0
    staged = staged and (width // 2) % 128 == 0 and (width // lon_count) % 16 == 0
    cot_met = lax.ppermute(cot_cols, "lat", swap_pairs(2, 1)) if staged else None

    beside = lat_rims(fields, met)
    beside = (*beside, *lon_rims(flags, beside, columns))
    h, packed = call(
        enter_kernel, "convolve_normalize_pack", [rows_shape, rows_shape],
        [pattern_row, fields, *beside, conv_kernel, gain],
        [pad, pltpu.VMEM((cells, width), bf16)], mib=BIG,
    )
    arrived = exchange(packed)
    half_shape = shape((width // 2, cells), bf16)
    grad_grouped, att, att_sent = pl.pallas_call(
        lambda *refs: attention_kernel(slots, blocks, UNROLL, *refs),
        name="attention",
        out_shape=[rows_shape, cols_shape, half_shape],
        in_specs=[ANY] * 4,
        out_specs=[ANY] * 3,
        scratch_shapes=[
            pltpu.VMEM((cells, width), bf16), pltpu.VMEM(qkv_weight.shape, bf16),
            pltpu.VMEM(bias.shape, f32), pltpu.VMEM((width, cells), bf16),
            pltpu.VMEM((width, cells), bf16), pltpu.VMEM((3 * width, cells), bf16),
            pltpu.VMEM((3 * width, cells), bf16), pltpu.SemaphoreType.DMA((4,)),
        ],
        compiler_params=pltpu.CompilerParams(vmem_limit_bytes=BIG * 1024 * 1024),
        cost_estimate=pl.CostEstimate(
            flops=12_000_000_000, bytes_accessed=8_000_000, transcendentals=0
        ),
    )(arrived, qkv_weight, bias, grad_att)
    grad_home = exchange(grad_grouped)
    mixed, project = attended_products(
        slots, blocks, cot_cols, cot_met, att, att_sent, out_weight
    )
    grad_home, mixed = lax.optimization_barrier((grad_home, mixed))
    mixed_home = exchange(mixed)

    grad_h, sums, message, columns = call(
        return_kernel, "normalize_back",
        [
            shape(fields.shape, bf16), shape((16, width), f32),
            shape((cols + 32, width), bf16), columns_shape,
        ],
        [pattern_row, grad_home, h, cot_rows, gain, fields, *beside],
        [pad, pltpu.VMEM((cells, width), f32)],
    )
    if lat_count == 2:
        met = lax.ppermute(message, "lat", swap_pairs(2, 1))
        sums = sums + one_term(met[cols:])
        beside = lat_rims(grad_h, met[:cols])
    else:
        sums = total_over("lat", sums)
        beside = lat_rims(grad_h, None)
    staged = isinstance(project, tuple)
    if staged:
        even, odd, met = lon_rims(flags, beside, columns, two_terms(sums))
        beside = (*beside, even, odd)
        sums = sums + one_term(met)
        sums = sums + lax.ppermute(sums, "lon", swap_pairs(lon_count, 2))
        kept, met = project
        bit = 4
        while bit < lon_count:
            if 2 * bit == lon_count:
                sums, odd, mixed_home = lax.optimization_barrier((sums, odd, mixed_home))
                beside = (*beside[:3], odd)
            project = (kept.astype(f32) + met.astype(f32)).astype(bf16)
            kept, sent = halved(project, bit)
            high_low = two_terms(sums).reshape(-1, sent.shape[-1])
            sent = sent.reshape(-1, sent.shape[-1])
            met = lax.ppermute(
                jnp.concatenate([high_low, sent], axis=0), "lon", swap_pairs(lon_count, bit)
            )
            sums = sums + one_term(met[: high_low.shape[0]].reshape(2 * sums.shape[0], width))
            met = met[high_low.shape[0] :].reshape(kept.shape)
            bit *= 2
        kept, met = kept[0], met[0]
    else:
        beside = (*beside, *lon_rims(flags, beside, columns))
        sums = total_over("lon", sums)
        kept, met = project, jnp.zeros_like(project)
    grad_fields = call(
        spread_kernel, "convolve_back", [shape(fields.shape, bf16)],
        [grad_h, *beside, conv_kernel], [pad],
    )[0]
    block_out = call(leave_kernel, "block_out", [rows_shape], [pattern_row, mixed_home, h])[0]
    grad_kernel, gain_gradient, grad_project = call(
        lambda *refs: finish_kernel(scale_everywhere, *refs), "finish",
        [shape((3, 3, width), f32), shape((width,), f32), shape(kept.shape, f32)],
        [sums, kept, met],
    )
    return (
        block_out.reshape(rows, cols, width),
        grad_fields,
        grad_project.T,
        grad_kernel,
        gain_gradient,
    )


def solution(mesh):
    placed = (
        P("lat", "lon", None),
        P(),
        P(),
        P(),
        P(),
        P(),
        P("lat", "lon", None),
        P("lat", "lon", None),
    )
    return jax.shard_map(
        body,
        mesh=mesh,
        in_specs=placed,
        out_specs=(P("lat", "lon", None), P("lat", "lon", None), P("lat", "lon"), P(), P()),
        check_vma=False,
    )
```

```python
import math

import jax
import jax.numpy as jnp
from jax import lax
from jax.experimental import pallas as pl
from jax.experimental.pallas import tpu as pltpu
from jax.sharding import PartitionSpec as P

HEADS = 24
HEAD_DIM = 32
GROUP = 64
PAIR = 2 * GROUP
EDGE = 8
UNROLL = 24

epsilon = 1e-05
f32, bf16 = jnp.float32, jnp.bfloat16
AXES = ("lat", "lon")
NN = (((1,), (0,)), ((), ()))
NT = (((1,), (1,)), ((), ()))
TN = (((0,), (0,)), ((), ()))
TT = (((0,), (1,)), ((), ()))
VMEM = pl.BlockSpec(memory_space=pltpu.VMEM)
SMEM = pl.BlockSpec(memory_space=pltpu.SMEM)
ANY = pl.BlockSpec(memory_space=pl.ANY)
BIG = 60


def dot(a, b, dims=NN):
    return lax.dot_general(a, b, dims, preferred_element_type=f32)


def whole(x):
    return pl.BlockSpec(x.shape, lambda step: (0,) * len(x.shape))


def call(kernel, name, out_shape, operands, scratch=(), flops=0, specs=(), mib=40):
    size = sum(math.prod(x.shape) * x.dtype.itemsize for x in (*operands, *out_shape))
    specs = dict(specs)
    return pl.pallas_call(
        kernel,
        name=name,
        grid=(1,),
        out_shape=list(out_shape),
        in_specs=[specs.get(i, whole(x)) for i, x in enumerate(operands)],
        out_specs=[whole(x) for x in out_shape],
        scratch_shapes=list(scratch),
        compiler_params=pltpu.CompilerParams(vmem_limit_bytes=mib * 1024 * 1024),
        cost_estimate=pl.CostEstimate(flops=flops, bytes_accessed=size, transcendentals=0),
    )(*operands)


def fetch(sems, *pairs):
    copies = [pltpu.make_async_copy(x, y, sems.at[i]) for i, (x, y) in enumerate(pairs)]
    for copy in copies:
        copy.start()
    return copies


def shape(dims, dtype):
    return jax.ShapeDtypeStruct(dims, dtype)


def place():
    lat, lon = lax.axis_index("lat"), lax.axis_index("lon")
    return lat, lax.axis_size("lat") - 1 - lat, lax.rem(lon, 2)


def by_cell(pattern_row, cells):
    cell = lax.broadcasted_iota(jnp.int32, (cells, cells), 0)
    return jnp.where(pattern_row == cell, 1.0, 0.0).astype(bf16)


def position_by_row(cells, slots, blocks, row_dim):
    row = lax.broadcasted_iota(jnp.int32, (cells, cells), row_dim)
    position = lax.broadcasted_iota(jnp.int32, (cells, cells), 1 - row_dim)
    place = lax.rem(row, slots) * blocks + lax.div(row, slots)
    return jnp.where(place == position, 1.0, 0.0).astype(bf16)


def rim_cells(field_ref, row_ref, cols_ref):
    rows, cols, _ = field_ref.shape
    low, even = place()[0] == 0, place()[2] == 0
    row_ref[...] = jnp.where(low, field_ref[rows - 1], field_ref[0])
    first = jnp.concatenate([field_ref[row, 0:1] for row in range(rows)], axis=0)
    last = jnp.concatenate([field_ref[row, cols - 1 : cols] for row in range(rows)], axis=0)
    cols_ref[0] = jnp.where(even, last, first)
    cols_ref[1] = jnp.where(even, first, last)


def start_kernel(pattern_ref, rows_ref, field_ref, out_ref, row_ref, cols_ref):
    cells = rows_ref.shape[0]
    rim_cells(field_ref, row_ref, cols_ref)
    out_ref[...] = dot(by_cell(pattern_ref[...], cells), rows_ref[...], TN).astype(bf16)


def fill_pad(pad, field_ref, before_ref, after_ref, even_ref, odd_ref):
    rows, cols, _ = field_ref.shape
    before, after = before_ref[...].astype(f32), after_ref[...].astype(f32)
    pad[0, EDGE : EDGE + cols] = jnp.where(place()[0] != 0, before, jnp.zeros_like(before))
    pad[rows + 1, EDGE : EDGE + cols] = jnp.where(place()[1] != 0, after, jnp.zeros_like(after))
    for row in range(rows):
        pad[row + 1, EDGE : EDGE + cols] = field_ref[row].astype(f32)
    even, odd = even_ref[...].astype(f32), odd_ref[...].astype(f32)
    left = jnp.where(place()[2] == 0, odd, even)
    right = jnp.where(place()[2] == 0, even, odd)
    for row in range(rows + 2):
        pad[row, EDGE - 1 : EDGE] = left[row : row + 1]
        pad[row, EDGE + cols : EDGE + cols + 1] = right[row : row + 1]


def taps_row(pad, taps, row, cols, flip):
    summed = pad[row + 1, EDGE : EDGE + cols]
    for a in range(3):
        for b in range(3):
            tap = taps[2 - a, 2 - b : 3 - b] if flip else taps[a, b : b + 1]
            summed = summed + tap * pad[row + a, EDGE - 1 + b : EDGE - 1 + b + cols]
    return summed


def normalized(h):
    mean = jnp.mean(h, axis=-1, keepdims=True)
    centred = h - mean
    var = jnp.mean(centred * centred, axis=-1, keepdims=True)
    deviation = lax.rsqrt(var + epsilon)
    return centred * deviation, deviation


def enter_kernel(
    pattern_ref, field_ref, before_ref, after_ref, even_ref, odd_ref, taps_ref, gain_ref,
    h_ref, out_ref, pad, normed,
):
    rows, cols, _ = field_ref.shape
    fill_pad(pad, field_ref, before_ref, after_ref, even_ref, odd_ref)
    taps, gain = taps_ref[...], gain_ref[...]
    for row in range(rows):
        h = taps_row(pad, taps, row, cols, False).astype(bf16)
        h_ref[row * cols : (row + 1) * cols] = h
        xhat, _ = normalized(h.astype(f32))
        normed[row * cols : (row + 1) * cols] = (xhat * gain).astype(bf16)
    out_ref[...] = dot(by_cell(pattern_ref[...], rows * cols), normed[...], TN).astype(bf16)


def cot_kernel(slots, blocks, arrived_ref, out_weight_ref, grad_att_ref, cot_ref):
    cells = arrived_ref.shape[0]
    grouped = dot(position_by_row(cells, slots, blocks, 1), arrived_ref[...]).astype(bf16)
    grad_att_ref[...] = dot(out_weight_ref[...], grouped, NT).astype(bf16)
    cot_ref[...] = grouped.T


def low_lanes(dims):
    return lax.broadcasted_iota(jnp.int32, dims, len(dims) - 1) < GROUP


def pair_scores(left, right):
    both = dot(left, right, TN)
    return jnp.where(low_lanes((GROUP, PAIR)), both[:GROUP], both[GROUP:])


def pair_diagonal(compact):
    low = low_lanes((GROUP, PAIR))
    zero = jnp.zeros_like(compact)
    return jnp.concatenate([jnp.where(low, compact, zero), jnp.where(low, zero, compact)], axis=0)


def attention_kernel(
    slots, blocks, unroll,
    arrived_hbm, qkv_weight_hbm, bias_hbm, grad_att_hbm,
    grad_hbm, att_hbm, att_sent_hbm,
    rows_buffer, qkv_weight, bias, grad_att, att_ref, qkv, grad_qkv, sems,
):
    cells, width = rows_buffer.shape
    copies = fetch(
        sems,
        (arrived_hbm, rows_buffer), (qkv_weight_hbm, qkv_weight), (bias_hbm, bias), (grad_att_hbm, grad_att),
    )
    gather = position_by_row(cells, slots, blocks, 1)
    copies[0].wait()
    grouped = dot(gather, rows_buffer[...]).astype(bf16)
    copies[1].wait()
    step = width // 2
    for at in range(0, 3 * width, step):
        qkv[at : at + step] = dot(qkv_weight[:, at : at + step], grouped, TT).astype(bf16)
    copies[2].wait()
    copies[3].wait()
    scale = HEAD_DIM ** (-0.5)

    def heads(step, carry):
        some = [
            (step * unroll + u, slice(pair * PAIR, (pair + 1) * PAIR))
            for u in range(unroll)
            for pair in range(cells // PAIR)
        ]

        def rows(part, e):
            return pl.ds(pl.multiple_of(part * width + e * HEAD_DIM, HEAD_DIM), HEAD_DIM)

        def q(e, at):
            return qkv[rows(0, e), at]

        def k(e, at):
            return qkv[rows(1, e), at]

        def v(e, at):
            return qkv[rows(2, e), at]

        def grad(e, at):
            return grad_att[rows(0, e), at]

        scores = [pair_scores(k(*x), q(*x)) * scale + bias[x[0]] for x in some]
        grad_probs = [pair_scores(v(*x), grad(*x)) for x in some]
        lifted = [jnp.exp(y - jnp.max(y, axis=0, keepdims=True)) for y in scores]
        probs = [y / jnp.sum(y, axis=0, keepdims=True) for y in lifted]
        probs_low = [pair_diagonal(y).astype(bf16) for y in probs]
        att = [dot(v(*x), y) for x, y in zip(some, probs_low)]
        to_value = [dot(grad(*x), y, NT) for x, y in zip(some, probs_low)]
        grad_scores = []
        for y, z in zip(probs, grad_probs):
            product = y * z
            inner = product - y * jnp.sum(product, axis=0, keepdims=True)
            grad_scores.append(pair_diagonal(inner).astype(bf16))
        to_query = [dot(k(*x), y) * scale for x, y in zip(some, grad_scores)]
        to_key = [dot(q(*x), y, NT) * scale for x, y in zip(some, grad_scores)]
        for i, (e, at) in enumerate(some):
            att_ref[rows(0, e), at] = att[i].astype(bf16)
            grad_qkv[rows(0, e), at] = to_query[i].astype(bf16)
            grad_qkv[rows(1, e), at] = to_key[i].astype(bf16)
            grad_qkv[rows(2, e), at] = to_value[i].astype(bf16)
        return carry

    if unroll == HEADS:
        heads(0, 0)
    else:
        lax.fori_loop(0, HEADS // unroll, heads, 0)
    sent = att_sent_hbm.shape[0]
    other = pl.multiple_of((1 - jnp.minimum(place()[0], 1)) * sent, 16)
    leaving = fetch(sems, (att_ref.at[pl.ds(other, sent)], att_sent_hbm), (att_ref, att_hbm))
    grad = dot(qkv_weight[...], grad_qkv[...]).astype(bf16)
    rows_buffer[...] = dot(position_by_row(cells, slots, blocks, 0), grad, NT).astype(bf16)
    for copy in [*leaving, *fetch(sems.at[pl.ds(2, 1)], (rows_buffer, grad_hbm))]:
        copy.wait()


def mix(slots, blocks, out_weight_ref, att_ref, mixed_ref):
    mixed = dot(out_weight_ref[...], att_ref[...], TN).astype(bf16)
    scatter = position_by_row(att_ref.shape[1], slots, blocks, 0)
    mixed_ref[...] = dot(scatter, mixed, NT).astype(bf16)


def products_kernel(slots, blocks, cot_ref, att_ref, out_weight_ref, mixed_ref, out_ref):
    out_ref[...] = dot(cot_ref[...], att_ref[...], NT).astype(bf16)
    mix(slots, blocks, out_weight_ref, att_ref, mixed_ref)


def mix_kernel(slots, blocks, att_ref, out_weight_ref, mixed_ref):
    mix(slots, blocks, out_weight_ref, att_ref, mixed_ref)


def halves_kernel(cot_ref, cot_met_ref, att_ref, att_met_ref, kept_ref, sent_ref, part):
    chips, cols, rows = kept_ref.shape
    lat, _, core = place()
    mine = att_ref[pl.ds(pl.multiple_of(jnp.minimum(lat, 1) * rows, 16), rows)]
    total = dot(cot_ref[...], mine, NT) + dot(cot_met_ref[...], att_met_ref[...], NT)
    part[...] = total.astype(bf16)
    for chip in range(chips):
        kept_ref[chip] = part[pl.ds(pl.multiple_of((2 * chip + core) * cols, 16), cols)]
        sent_ref[chip] = part[pl.ds(pl.multiple_of((2 * chip + 1 - core) * cols, 16), cols)]


def leave_kernel(pattern_ref, mixed_ref, h_ref, out_ref):
    mixed = dot(by_cell(pattern_ref[...], h_ref.shape[0]), mixed_ref[...])
    out_ref[...] = (h_ref[...].astype(f32) + mixed).astype(bf16)


def return_kernel(
    pattern_ref, arrived_ref, h_ref, cot_ref, gain_ref,
    field_ref, before_ref, after_ref, even_ref, odd_ref,
    grad_ref, sums_ref, message_ref, columns_ref, pad, normed_grad,
):
    rows, cols, width = field_ref.shape
    fill_pad(pad, field_ref, before_ref, after_ref, even_ref, odd_ref)
    normed_grad[...] = dot(by_cell(pattern_ref[...], rows * cols), arrived_ref[...])
    gain = gain_ref[...]

    def fold(x):
        return jnp.sum(x.reshape(cols // 8, 8, width), axis=0)

    sums = [jnp.zeros((8, width), f32) for _ in range(10)]
    for row in range(rows):
        at = slice(row * cols, (row + 1) * cols)
        xhat, deviation = normalized(h_ref[at].astype(f32))
        grad = normed_grad[at]
        sums[9] = sums[9] + fold(grad * xhat)
        u = grad * gain
        inner = u - jnp.mean(u, axis=-1, keepdims=True)
        inner = inner - xhat * jnp.mean(u * xhat, axis=-1, keepdims=True)
        grad_h = (cot_ref[at].astype(f32) + deviation * inner).astype(bf16)
        grad_ref[row] = grad_h
        grad_h = grad_h.astype(f32)
        for a in range(3):
            for b in range(3):
                moved = pad[row + a, EDGE - 1 + b : EDGE - 1 + b + cols]
                sums[3 * a + b] = sums[3 * a + b] + fold(moved * grad_h)
    for i in range(10):
        sums_ref[i : i + 1] = jnp.sum(sums[i], axis=0, keepdims=True)
    sums_ref[10:16] = jnp.zeros((6, width), f32)
    rim_cells(grad_ref, message_ref.at[:cols], columns_ref)
    total = sums_ref[...]
    high = total.astype(bf16)
    message_ref[cols : cols + 16] = high
    message_ref[cols + 16 :] = (total - high.astype(f32)).astype(bf16)


def finish_kernel(scale, sums_ref, kept_ref, met_ref, taps_ref, gain_ref, project_ref):
    sums = sums_ref[...] * scale
    for a in range(3):
        taps_ref[a] = sums[3 * a : 3 * a + 3]
    gain_ref[...] = sums[9]
    project_ref[...] = (kept_ref[...].astype(f32) + met_ref[...].astype(f32)) * scale


def spread_kernel(
    field_ref, before_ref, after_ref, even_ref, odd_ref, taps_ref, out_ref, pad
):
    rows, cols, _ = field_ref.shape
    fill_pad(pad, field_ref, before_ref, after_ref, even_ref, odd_ref)
    taps = taps_ref[...]
    for row in range(rows):
        out_ref[row] = taps_row(pad, taps, row, cols, True).astype(bf16)


def swap_pairs(size, bit):
    return [(i, i ^ bit) for i in range(size)]


def lat_rims(field, met):
    if lax.axis_size("lat") == 2:
        return met, met
    up = [(i, i + 1) for i in range(lax.axis_size("lat") - 1)]
    before = lax.ppermute(field[-1], "lat", up)
    after = lax.ppermute(field[0], "lat", [(j, i) for i, j in up])
    return before, after


def lon_rims(flags, rows, columns, riders=None):
    lon_count = lax.axis_size("lon")
    before, after = rows
    even = flags[2] == 0

    def column(which, last):
        at = before.shape[0] - 1

        def corner(row, there):
            cell = jnp.where(last, row[at:], row[:1])
            return jnp.where(there, cell, jnp.zeros_like(cell))

        return jnp.concatenate(
            [corner(before, flags[0] != 0), columns[which], corner(after, flags[1] != 0)], axis=0
        )

    sent = column(0, even)
    if riders is not None:
        sent = jnp.concatenate([riders, sent], axis=0)
    met_even = lax.ppermute(sent, "lon", swap_pairs(lon_count, 1))
    odd_pairs = [(i, (i + 1 if i % 2 else i - 1) % lon_count) for i in range(lon_count)]
    met_odd = lax.ppermute(column(1, jnp.logical_not(even)), "lon", odd_pairs)
    if riders is None:
        return met_even, met_odd
    count = riders.shape[0]
    return met_even[count:], met_odd, met_even[:count]


def exchange(rows):
    blocks = lax.axis_size("lat") * lax.axis_size("lon")
    cells, width = rows.shape
    sent = rows.reshape(blocks, cells // blocks, width)
    return lax.all_to_all(sent, AXES, split_axis=0, concat_axis=0, tiled=True).reshape(cells, width)


def attended_products(slots, blocks, cot_cols, cot_met, att, att_sent, out_weight):
    width, cells = att.shape
    lat_count, lon_count = lax.axis_size("lat"), lax.axis_size("lon")
    rows, cols = width // lat_count, width // lon_count
    mixed_shape = shape((cells, width), bf16)
    if cot_met is None:
        mixed, parts = call(
            lambda *refs: products_kernel(slots, blocks, *refs),
            "attended_products", [mixed_shape, shape((width, width), bf16)],
            [cot_cols, att, out_weight],
        )
        parts = parts.reshape(lon_count, cols, lat_count, rows).transpose(2, 0, 1, 3)
        parts = parts.reshape(lat_count * lon_count, cols, rows)
        parts = lax.all_to_all(parts, AXES, split_axis=0, concat_axis=0, tiled=True)
        return mixed, jnp.sum(parts.astype(f32), axis=0)
    mixed = call(
        lambda *refs: mix_kernel(slots, blocks, *refs), "mix", [mixed_shape], [att, out_weight]
    )[0]
    att_met = lax.ppermute(att_sent, "lat", swap_pairs(2, 1))
    halves = shape((lon_count // 2, cols, rows), bf16)
    kept, sent = call(
        halves_kernel, "project_gradient", [halves, halves], [cot_cols, cot_met, att, att_met],
        [pltpu.VMEM((width, rows), bf16)],
    )
    met = lax.ppermute(sent, "lon", swap_pairs(lon_count, 1))
    parts = (kept.astype(f32) + met.astype(f32)).astype(bf16)
    kept, sent = halved(parts, 2)
    return mixed, (kept, lax.ppermute(sent, "lon", swap_pairs(lon_count, 2)))


def halved(parts, bit):
    mine = lax.rem(lax.div(lax.axis_index("lon"), bit), 2)
    pairs = parts.reshape(parts.shape[0] // 2, 2, *parts.shape[1:])
    kept = lax.dynamic_index_in_dim(pairs, mine, 1, keepdims=False)
    return kept, lax.dynamic_index_in_dim(pairs, 1 - mine, 1, keepdims=False)


def two_terms(x):
    high = x.astype(bf16)
    return jnp.concatenate([high, (x - high.astype(f32)).astype(bf16)], axis=0)


def one_term(x):
    half = x.shape[0] // 2
    return x[:half].astype(f32) + x[half:].astype(f32)


def total_over(axis, x):
    size, bit = lax.axis_size(axis), 1
    if size & (size - 1):
        return lax.psum(x, axis)
    while bit < size:
        x = x + lax.ppermute(x, axis, swap_pairs(size, bit))
        bit *= 2
    return x


def body(
    fields, conv_kernel, layer_norm_gain, qkv_weight, out_weight, score_bias, pattern, cotangent
):
    rows, cols, width = fields.shape
    cells = rows * cols
    lat_count, lon_count = lax.axis_size("lat"), lax.axis_size("lon")
    blocks = lat_count * lon_count
    slots = cells // blocks
    scale_everywhere = 1.0 / math.sqrt(cells * blocks)
    pattern_row = pattern.reshape(1, cells)
    gain = layer_norm_gain.reshape(1, width)
    cot_rows = cotangent.reshape(cells, width)
    bias = jnp.swapaxes(score_bias, 1, 2)
    bias = jnp.concatenate([bias, bias], axis=2)
    pad = pltpu.VMEM((rows + 2, cols + 2 * EDGE, width), f32)
    rows_shape = shape((cells, width), bf16)
    cols_shape = shape((width, cells), bf16)
    tall_shape = shape((3 * width, cells), bf16)

    flags = (
        lax.axis_index("lat"), lat_count - 1 - lax.axis_index("lat"), lax.rem(lax.axis_index("lon"), 2)
    )
    row_shape, columns_shape = shape((cols, width), bf16), shape((2, rows, width), bf16)

    cot_packed, row, columns = call(
        start_kernel, "start", [rows_shape, row_shape, columns_shape],
        [pattern_row, cot_rows, fields], mib=BIG,
    )
    met = lax.ppermute(row, "lat", swap_pairs(2, 1)) if lat_count == 2 else None
    cot_arrived = exchange(cot_packed)
    grad_att, cot_cols = call(
        lambda *refs: cot_kernel(slots, blocks, *refs),
        "cotangent_products", [cols_shape, cols_shape], [cot_arrived, out_weight], mib=BIG,
    )

    staged = lat_count == 2 and lon_count % 4 == 0 and lon_count & (lon_count - 1) == 0
    staged = staged and (width // 2) % 128 == 0 and (width // lon_count) % 16 == 0
    cot_met = lax.ppermute(cot_cols, "lat", swap_pairs(2, 1)) if staged else None

    beside = lat_rims(fields, met)
    beside = (*beside, *lon_rims(flags, beside, columns))
    h, packed = call(
        enter_kernel, "convolve_normalize_pack", [rows_shape, rows_shape],
        [pattern_row, fields, *beside, conv_kernel, gain],
        [pad, pltpu.VMEM((cells, width), bf16)], mib=BIG,
    )
    arrived = exchange(packed)
    half_shape = shape((width // 2, cells), bf16)
    grad_grouped, att, att_sent = pl.pallas_call(
        lambda *refs: attention_kernel(slots, blocks, UNROLL, *refs),
        name="attention",
        out_shape=[rows_shape, cols_shape, half_shape],
        in_specs=[ANY] * 4,
        out_specs=[ANY] * 3,
        scratch_shapes=[
            pltpu.VMEM((cells, width), bf16), pltpu.VMEM(qkv_weight.shape, bf16),
            pltpu.VMEM(bias.shape, f32), pltpu.VMEM((width, cells), bf16),
            pltpu.VMEM((width, cells), bf16), pltpu.VMEM((3 * width, cells), bf16),
            pltpu.VMEM((3 * width, cells), bf16), pltpu.SemaphoreType.DMA((4,)),
        ],
        compiler_params=pltpu.CompilerParams(vmem_limit_bytes=BIG * 1024 * 1024),
        cost_estimate=pl.CostEstimate(
            flops=12_000_000_000, bytes_accessed=8_000_000, transcendentals=0
        ),
    )(arrived, qkv_weight, bias, grad_att)
    grad_home = exchange(grad_grouped)
    mixed, project = attended_products(
        slots, blocks, cot_cols, cot_met, att, att_sent, out_weight
    )
    grad_home, mixed = lax.optimization_barrier((grad_home, mixed))
    mixed_home = exchange(mixed)

    grad_h, sums, message, columns = call(
        return_kernel, "normalize_back",
        [
            shape(fields.shape, bf16), shape((16, width), f32),
            shape((cols + 32, width), bf16), columns_shape,
        ],
        [pattern_row, grad_home, h, cot_rows, gain, fields, *beside],
        [pad, pltpu.VMEM((cells, width), f32)],
    )
    if lat_count == 2:
        met = lax.ppermute(message, "lat", swap_pairs(2, 1))
        sums = sums + one_term(met[cols:])
        beside = lat_rims(grad_h, met[:cols])
    else:
        sums = total_over("lat", sums)
        beside = lat_rims(grad_h, None)
    staged = isinstance(project, tuple)
    if staged:
        even, odd, met = lon_rims(flags, beside, columns, two_terms(sums))
        beside = (*beside, even, odd)
        sums = sums + one_term(met)
        sums = sums + lax.ppermute(sums, "lon", swap_pairs(lon_count, 2))
        sums = sums[:10]
        kept, met = project
        bit = 4
        while bit < lon_count:
            if 2 * bit == lon_count:
                sums, odd, mixed_home = lax.optimization_barrier((sums, odd, mixed_home))
                beside = (*beside[:3], odd)
            project = (kept.astype(f32) + met.astype(f32)).astype(bf16)
            kept, sent = halved(project, bit)
            high_low = two_terms(sums).reshape(-1, sent.shape[-1])
            sent = sent.reshape(-1, sent.shape[-1])
            met = lax.ppermute(
                jnp.concatenate([high_low, sent], axis=0), "lon", swap_pairs(lon_count, bit)
            )
            sums = sums + one_term(met[: high_low.shape[0]].reshape(2 * sums.shape[0], width))
            met = met[high_low.shape[0] :].reshape(kept.shape)
            bit *= 2
        kept, met = kept[0], met[0]
    else:
        beside = (*beside, *lon_rims(flags, beside, columns))
        sums = total_over("lon", sums)
        kept, met = project, jnp.zeros_like(project)
    grad_fields = call(
        spread_kernel, "convolve_back", [shape(fields.shape, bf16)],
        [grad_h, *beside, conv_kernel], [pad],
    )[0]
    block_out = call(leave_kernel, "block_out", [rows_shape], [pattern_row, mixed_home, h])[0]
    grad_kernel, gain_gradient, grad_project = call(
        lambda *refs: finish_kernel(scale_everywhere, *refs), "finish",
        [shape((3, 3, width), f32), shape((width,), f32), shape(kept.shape, f32)],
        [sums, kept, met],
    )
    return (
        block_out.reshape(rows, cols, width),
        grad_fields,
        grad_project.T,
        grad_kernel,
        gain_gradient,
    )


def solution(mesh):
    placed = (
        P("lat", "lon", None),
        P(),
        P(),
        P(),
        P(),
        P(),
        P("lat", "lon", None),
        P("lat", "lon", None),
    )
    return jax.shard_map(
        body,
        mesh=mesh,
        in_specs=placed,
        out_specs=(P("lat", "lon", None), P("lat", "lon", None), P("lat", "lon"), P(), P()),
        check_vma=False,
    )
```
